256 devices in a mesh: pool: 4 (over x), seq: 8 (over y, core), tp: 8 (over z).
Axes of the slice: x: 4, y: 4, z: 8, core: 2. Of those that a mesh axis runs over, the one named last changes fastest.
Arguments:
- prior_cache: bfloat16 [16, 8192, 8, 2, 128], P(None, ('pool', 'seq'), 'tp'), may hold values from -16 to 16
- prefix_length: int32 [16], replicated, may hold values from 2048 to 8192, as said below
- slot_trace: int32 [16], replicated, may hold values from 0 to 15, each once
- queries: bfloat16 [16, 128, 8, 8, 128], P('seq', None, 'tp', 'pool'), may hold values from -16 to 16
- new_token_cache: bfloat16 [16, 128, 8, 2, 128], P('seq', None, 'tp'), may hold values from -6 to 6
- boundaries: int32 [16, 16], P('seq'), may hold values from 0 to 127, as said below
- output_weight: bfloat16 [8, 8, 128, 8192], P('tp', 'pool'), may hold values from -0.75 to 0.75
- reward_weight: float32 [8192], P(('pool', 'tp')), may hold values from -0.0625 to 0.0625
Outputs:
- layer_out: bfloat16 [16, 128, 8192], P('seq', None, ('pool', 'tp'))
- rewards: float32 [16, 16], P('seq')
The draws below stay inside these ranges and needn't reach their ends.
Inputs may be any that keep to these rules, and one draw needn't show every extreme that they name: `slot_trace`: a permutation; slot j belongs to scoring group j // 2. `prefix_length`: one trace has exactly 8192 valid positions and another exactly 2048. `boundaries`: each row rises strictly and ends with 127.
All inputs are finite; a program needn't handle non-finite values.
Results may differ from the reference program's by a relative error of at most 0.0085.
Values may be sent and summed in bfloat16 or wider, within the bound.
No kernel may reach another device: no remote copies, remote signals or barrier semaphores. Data moves between devices by JAX's collectives and lax.ppermute only.
A program may use at most 128 MiB of HBM per device.

```python
import jax
import jax.numpy as jnp
from jax import lax

MODEL_WIDTH = 8192
QUERY_HEADS = 64
KEY_HEADS = 8
HEAD_SIZE = 128
STEPS = 16
QUERY_PER_KV = 8
TRACE_COUNT = 16
PREFIX_LENGTH = 8192
NEW_TOKENS = 128


def draw_prior_cache(key, part):
    key = jax.random.fold_in(key, 11)
    array_shape = (TRACE_COUNT, PREFIX_LENGTH, KEY_HEADS, 2, HEAD_SIZE)
    values = jnp.clip(jax.random.normal(key, array_shape, jnp.float32), -4.0, 4.0)
    return values.astype(jnp.bfloat16)


def draw_queries(key, part):
    key = jax.random.fold_in(key, 3)
    array_shape = (TRACE_COUNT, NEW_TOKENS, KEY_HEADS, QUERY_PER_KV, HEAD_SIZE)
    values = jnp.clip(2.0 * jax.random.normal(key, array_shape, jnp.float32), -8.0, 8.0)
    return values.astype(jnp.bfloat16)


def draw_prefix_length(key, part):
    key = jax.random.fold_in(key, 5)
    first_key, second_key = jax.random.split(key)
    lengths = jax.random.randint(first_key, (TRACE_COUNT,), PREFIX_LENGTH // 4, PREFIX_LENGTH + 1)
    shuffled = jax.random.permutation(second_key, TRACE_COUNT)
    indices = jnp.arange(TRACE_COUNT)
    lengths = jnp.where(indices == shuffled[0], PREFIX_LENGTH, lengths)
    lengths = jnp.where(indices == shuffled[1], PREFIX_LENGTH // 4, lengths)
    return lengths.astype(jnp.int32)


def draw_boundaries(key, part):
    key = jax.random.fold_in(key, 7)
    slot_keys = jax.random.split(key, TRACE_COUNT)

    def one_row(row_key):
        picks = jax.random.permutation(row_key, NEW_TOKENS - 1)[:STEPS - 1]
        return jnp.concatenate([jnp.sort(picks), jnp.full((1,), NEW_TOKENS - 1, picks.dtype)])
    return jax.vmap(one_row)(slot_keys).astype(jnp.int32)


def shard_levels(stream_key, shape, cuts, smallest, top_value):
    factor_of, own = 1.0, jax.random.fold_in(stream_key, 6)
    for dim, shards_of in cuts:
        heights = jnp.exp(jax.random.uniform(jax.random.fold_in(own, dim), (shards_of,), jnp.float32, smallest / len(cuts), top_value / len(cuts)))
        factor_of = factor_of * jnp.repeat(heights, shape[dim] // shards_of).reshape([-1 if axis == dim else 1 for axis in range(len(shape))])
    return factor_of


def noise(own_key, shape, spread, limit, cuts=(), held_as=jnp.bfloat16):
    loudness = shard_levels(own_key, shape, cuts, -0.22, 0.18) if cuts else 1.0
    values = jax.random.normal(own_key, shape, jnp.float32) * spread * loudness
    return jnp.minimum(jnp.maximum(values, -limit), limit).astype(held_as)


def setup_inputs(seed: int = 0) -> dict:
    keys = jax.random.split(jax.random.key(seed), 9)
    return {
        "prior_cache": draw_prior_cache(jax.random.fold_in(keys[8], 71), 0),
        "prefix_length": draw_prefix_length(jax.random.fold_in(keys[8], 71), 0),
        "slot_trace": jax.random.permutation(keys[2], TRACE_COUNT).astype(jnp.int32),
        "queries": draw_queries(jax.random.fold_in(keys[8], 71), 0),
        "new_token_cache": noise(keys[4], (TRACE_COUNT, NEW_TOKENS, KEY_HEADS, 2, HEAD_SIZE), 1.0, 6.0, ((0, 8), (2, 8))),
        "boundaries": draw_boundaries(jax.random.fold_in(keys[8], 71), 0),
        "output_weight": noise(keys[6], (KEY_HEADS, QUERY_PER_KV, HEAD_SIZE, MODEL_WIDTH), (QUERY_HEADS * HEAD_SIZE // 128) ** -0.5, 0.75, ((0, 8), (1, 4))),
        "reward_weight": noise(keys[7], (MODEL_WIDTH,), MODEL_WIDTH ** -0.5, 0.0625, ((0, 32),), jnp.float32),
    }


negative_fill = -1.0e30


def reference(prior_cache, prefix_length, slot_trace, queries, new_token_cache, boundaries, output_weight, reward_weight):
    scaling = HEAD_SIZE ** -0.5
    positions = jnp.arange(PREFIX_LENGTH)
    steps_seen = jnp.arange(NEW_TOKENS)
    causal = steps_seen[None, :] <= steps_seen[:, None]
    weight_rows = output_weight.reshape(QUERY_HEADS * HEAD_SIZE, MODEL_WIDTH)

    def one_slot(item):
        queried, fresh, trace = item
        prior = lax.dynamic_index_in_dim(prior_cache, trace, 0, keepdims=False)
        length = lax.dynamic_index_in_dim(prefix_length, trace, 0, keepdims=False)
        usable = positions < length

        def one_head(head_item):
            head_query, head_prior, head_fresh = head_item
            query_wide = head_query.astype(jnp.float32)
            prior_scores = jnp.einsum("igd,cd->gic", query_wide, head_prior[:, 0].astype(jnp.float32)) * scaling
            fresh_scores = jnp.einsum("igd,jd->gij", query_wide, head_fresh[:, 0].astype(jnp.float32)) * scaling
            prior_scores = jnp.where(usable[None, None, :], prior_scores, negative_fill)
            fresh_scores = jnp.where(causal[None], fresh_scores, negative_fill)
            peaks = jnp.maximum(jnp.max(prior_scores, -1), jnp.max(fresh_scores, -1))
            prior_weights = jnp.where(usable[None, None, :], jnp.exp(prior_scores - peaks[..., None]), 0.0)
            fresh_weights = jnp.where(causal[None], jnp.exp(fresh_scores - peaks[..., None]), 0.0)
            totals = jnp.sum(prior_weights, -1) + jnp.sum(fresh_weights, -1)
            prior_short = lax.optimization_barrier(prior_weights.astype(jnp.bfloat16))
            fresh_short = lax.optimization_barrier(fresh_weights.astype(jnp.bfloat16))
            blended = jnp.einsum("gic,cd->igd", prior_short.astype(jnp.float32), head_prior[:, 1].astype(jnp.float32))
            blended = blended + jnp.einsum("gij,jd->igd", fresh_short.astype(jnp.float32), head_fresh[:, 1].astype(jnp.float32))
            return (blended / jnp.transpose(totals)[:, :, None]).astype(jnp.bfloat16)

        heads_out = lax.map(one_head, (jnp.moveaxis(queried, 1, 0), jnp.moveaxis(prior, 1, 0), jnp.moveaxis(fresh, 1, 0)))
        attended = jnp.moveaxis(heads_out, 0, 1).reshape(NEW_TOKENS, QUERY_HEADS * HEAD_SIZE)
        return jnp.dot(attended, weight_rows, preferred_element_type=jnp.float32).astype(jnp.bfloat16)

    layer_out = lax.map(one_slot, (queries, new_token_cache, slot_trace.astype(jnp.int32)))
    picked = jnp.take_along_axis(layer_out, boundaries.astype(jnp.int32)[:, :, None], axis=1)
    rewards = jnp.einsum("jsd,d->js", picked.astype(jnp.float32), reward_weight.astype(jnp.float32))
    return layer_out, rewards
```

```python
import functools

import jax
import jax.numpy as jnp
from jax import lax
from jax.experimental import pallas as pl
from jax.experimental.pallas import tpu as pltpu
from jax.sharding import PartitionSpec as P

negative_fill = -1e30
peak_floor = -1e25
log2_e = 1.4426950408889634
VMEM = pl.BlockSpec(memory_space=pltpu.VMEM)
SMEM = pl.BlockSpec(memory_space=pltpu.SMEM)
ANY = pl.BlockSpec(memory_space=pl.ANY)
STAT_ROWS = 16


def kernel_params(mib):
    return pltpu.CompilerParams(vmem_limit_bytes=mib * 1024 * 1024)


def order_kernel(order_ref, cache_ref, *refs):
    outs, (held, wide, sems) = refs[:-3], refs[-3:]
    blocks, rows = held.shape[0], held.shape[1]
    per_part = blocks // len(outs)
    copies = [
        pltpu.make_async_copy(cache_ref.at[order_ref[n]], held.at[n], sems.at[n])
        for n in range(blocks)
    ]
    for copy in copies:
        copy.start()
    for n, copy in enumerate(copies):
        copy.wait()
        wide[...] = held[n].astype(jnp.float32)
        out = outs[n // per_part]
        for kind in range(2):
            out[n % per_part, kind] = wide[pl.ds(kind, rows // 2, stride=2), :].astype(jnp.bfloat16)


def order_blocks(prior_rows, order, parts):
    blocks, rows, size = prior_rows.shape
    return pl.pallas_call(
        order_kernel,
        out_shape=[
            jax.ShapeDtypeStruct((blocks // parts, 2, rows // 2, size), jnp.bfloat16)
            for _ in range(parts)
        ],
        in_specs=[SMEM, ANY],
        out_specs=[VMEM] * parts,
        scratch_shapes=[
            pltpu.VMEM((blocks, rows, size), jnp.bfloat16),
            pltpu.VMEM((rows, size), jnp.float32),
            pltpu.SemaphoreType.DMA((blocks,)),
        ],
        compiler_params=kernel_params(16),
    )(order, prior_rows)


def attend_kernel(info_ref, q0, q1, q2, q3, prior_ref, fresh_ref, p0, p1, p2, p3):
    valid = info_ref[0]
    sources, _, block, size = prior_ref.shape
    width = sources * block
    factor = size**-0.5 * log2_e
    keys = prior_ref[:, 0].reshape(width, size)
    values = prior_ref[:, 1].reshape(width, size)
    rows = q0.shape[0]
    usable = lax.broadcasted_iota(jnp.int32, (1, width), 1) < valid
    contract = (((1,), (1,)), ((), ()))
    for tile, (query, pay) in enumerate(((q0, p0), (q1, p1), (q2, p2), (q3, p3))):
        scores = lax.dot_general(query[...], keys, contract, preferred_element_type=jnp.float32)
        scores = jnp.where(usable, scores, negative_fill)
        peak = jnp.max(scores, -1, keepdims=True)
        if tile == 0:
            fresh_scores = lax.dot_general(
                query[...], fresh_ref[0], contract, preferred_element_type=jnp.float32
            )
            new_len = fresh_scores.shape[1]
            token = lax.rem(lax.broadcasted_iota(jnp.int32, fresh_scores.shape, 0), new_len)
            causal = lax.broadcasted_iota(jnp.int32, fresh_scores.shape, 1) <= token
            fresh_scores = jnp.where(causal, fresh_scores, negative_fill)
            peak = jnp.maximum(peak, jnp.max(fresh_scores, -1, keepdims=True))
        peak = jnp.maximum(peak * factor, peak_floor).astype(jnp.bfloat16).astype(jnp.float32)
        weights = jnp.exp2(scores * factor - peak)
        total = jnp.sum(weights, -1, keepdims=True)
        blended = jnp.dot(
            weights.astype(jnp.bfloat16), values, preferred_element_type=jnp.float32
        )
        if tile == 0:
            fresh_weights = jnp.exp2(fresh_scores * factor - peak)
            total = total + jnp.sum(fresh_weights, -1, keepdims=True)
            blended = blended + jnp.dot(
                fresh_weights.astype(jnp.bfloat16), fresh_ref[1], preferred_element_type=jnp.float32
            )
        pay[pl.ds(0, rows), :] = blended.astype(jnp.bfloat16)
        high = total.astype(jnp.bfloat16).astype(jnp.float32)
        low = total - high
        lane = lax.broadcasted_iota(jnp.int32, (rows, size), 1)
        stats = jnp.where(lane == 0, peak, jnp.where(lane == 1, high, jnp.where(lane == 2, low, 0.0)))
        halves = [stats[at : at + size].T[:8] for at in range(0, rows, size)]
        pay[pl.ds(rows, 8 * len(halves)), :] = jnp.concatenate(halves, 0).astype(jnp.bfloat16)


def attend(valid, queried, prior, fresh):
    rows, size = queried[0].shape
    pay = jax.ShapeDtypeStruct((rows + STAT_ROWS, size), jnp.bfloat16)
    return pl.pallas_call(
        attend_kernel,
        out_shape=[pay] * 4,
        in_specs=[SMEM] + [VMEM] * 6,
        out_specs=[VMEM] * 4,
        compiler_params=kernel_params(48),
    )(valid, *queried, prior, fresh)


def merge_kernel(p0, p1, p2, p3, out_ref):
    rows, size = out_ref.shape
    peaks, totals = [], []
    for pay in (p0, p1, p2, p3):
        stats = pay[pl.ds(rows, STAT_ROWS), :].astype(jnp.float32)
        columns = [
            jnp.concatenate([stats[8 * n : 8 * n + 8]] * (size // 8), 0).T
            for n in range(rows // size)
        ]
        columns = jnp.concatenate(columns, 0)
        peaks.append(columns[:, 0:1])
        totals.append(columns[:, 1:2] + columns[:, 2:3])
    top = functools.reduce(jnp.maximum, peaks)
    shares = [jnp.exp2(peak - top) for peak in peaks]
    total = sum(share * part for share, part in zip(shares, totals))
    blended = sum(
        share * pay[pl.ds(0, rows), :].astype(jnp.float32)
        for share, pay in zip(shares, (p0, p1, p2, p3))
    )
    out_ref[...] = (blended / total).astype(jnp.bfloat16)


def merge(pays):
    rows, size = pays[0].shape
    return pl.pallas_call(
        merge_kernel,
        out_shape=jax.ShapeDtypeStruct((rows - STAT_ROWS, size), jnp.bfloat16),
        in_specs=[VMEM] * 4,
        out_specs=VMEM,
        compiler_params=kernel_params(16),
    )(*pays)


def project_kernel(core_ref, *refs):
    attended, weights, out_ref = refs[:4], refs[4:12], refs[12]
    core = core_ref[0]
    tokens, wide = out_ref.shape[1], out_ref.shape[2]
    firsts = [ref[pl.ds(pl.multiple_of(core * tokens, tokens), tokens), :] for ref in attended]
    seconds = [ref[pl.ds(pl.multiple_of((1 - core) * tokens, tokens), tokens), :] for ref in attended]
    for dest in range(out_ref.shape[0]):
        at = pl.ds(dest * wide, wide)
        total = jnp.zeros((tokens, wide), jnp.float32)
        for n in range(4):
            total += jnp.dot(firsts[n], weights[2 * n][:, at], preferred_element_type=jnp.float32)
            total += jnp.dot(
                seconds[n], weights[2 * n + 1][:, at], preferred_element_type=jnp.float32
            )
        out_ref[dest] = total.astype(jnp.bfloat16)


def project(core, attended, weights, dests):
    rows, size = attended[0].shape
    columns = weights[0].shape[1]
    return pl.pallas_call(
        project_kernel,
        out_shape=jax.ShapeDtypeStruct((dests, rows // 2, columns // dests), jnp.bfloat16),
        in_specs=[SMEM] + [VMEM] * 12,
        out_specs=VMEM,
        compiler_params=kernel_params(32),
    )(core, *attended, *weights)


def shards(
    prior_cache,
    prefix_length,
    slot_trace,
    queries,
    new_token_cache,
    boundaries,
    output_weight,
    reward_weight,
):
    pool, seq, tp = lax.axis_index("pool"), lax.axis_index("seq"), lax.axis_index("tp")
    pools, seqs, tps = lax.axis_size("pool"), lax.axis_size("seq"), lax.axis_size("tp")
    slots, new_len, _, pair, size = queries.shape
    traces, block = prior_cache.shape[:2]
    core = lax.rem(seq, 2)
    core_arg = core.reshape(1).astype(jnp.int32)

    def from_pool(array, offset):
        return lax.ppermute(array, "pool", [((n + offset) % pools, n) for n in range(pools)])

    def swap_core(array):
        return lax.ppermute(array, "seq", [(n, n ^ 1) for n in range(seqs)])

    own_queries = jnp.transpose(queries[:, :, 0], (0, 2, 1, 3)).reshape(slots, pair * new_len, size)
    queried = [own_queries] + [from_pool(own_queries, o) for o in range(1, pools)]

    order = slot_trace.reshape(seqs, slots).T.reshape(-1)
    ordered = order_blocks(prior_cache.reshape(traces, 2 * block, size), order, slots)
    priors = [lax.all_to_all(part, "seq", split_axis=0, concat_axis=0, tiled=True) for part in ordered]

    rows_all = output_weight.reshape(pair * size, -1)
    columns = rows_all.shape[1] // pools

    def weight_block(half, column_block):
        return lax.dynamic_slice(rows_all, (half * size, column_block * columns), (size, columns))

    weights = [weight_block(core, pool), weight_block(1 - core, pool)]
    for o in range(1, pools):
        got = from_pool(weight_block(core, lax.rem(pool + pools - o, pools)), o)
        weights += [got, swap_core(got)]

    lengths = prefix_length[slot_trace]
    fresh = jnp.transpose(new_token_cache[:, :, 0], (0, 2, 1, 3))
    outs = []
    for slot in range(slots):
        length = lax.dynamic_slice(lengths, (seq * slots + slot,), (1,))
        valid = length - pool * seqs * block
        pays = attend(valid, [q[slot] for q in queried], priors[slot], fresh[slot])
        pays = [pays[0]] + [
            lax.ppermute(pays[o], "pool", [(n, (n + o) % pools) for n in range(pools)])
            for o in range(1, pools)
        ]
        attended = merge(pays)
        everyone = [attended] + [from_pool(attended, o) for o in range(1, pools)]
        partial = project(core_arg, everyone, weights, tps)
        arrived = lax.all_to_all(partial, "tp", split_axis=0, concat_axis=0, tiled=True)
        outs.append(jnp.sum(arrived.astype(jnp.float32), 0).astype(jnp.bfloat16))
    layer_out = jnp.stack(outs)
    picked = jnp.take_along_axis(layer_out, boundaries[:, :, None], axis=1)
    partial_rewards = jnp.sum(picked.astype(jnp.float32) * reward_weight, -1)
    spread = jnp.broadcast_to(partial_rewards, (pools * tps,) + partial_rewards.shape)
    rewards = jnp.sum(
        lax.all_to_all(spread, ("pool", "tp"), split_axis=0, concat_axis=0, tiled=True), 0
    )
    return (layer_out, rewards)


def solution(mesh):
    placed = (
        P(None, ("pool", "seq"), "tp", None, None),
        P(),
        P(),
        P("seq", None, "tp", "pool", None),
        P("seq", None, "tp", None, None),
        P("seq", None),
        P("tp", "pool", None, None),
        P(("pool", "tp")),
    )
    return jax.shard_map(
        shards,
        mesh=mesh,
        in_specs=placed,
        out_specs=(P("seq", None, ("pool", "tp")), P("seq", None)),
        check_vma=False,
    )
```

```python
import functools

import jax
import jax.numpy as jnp
from jax import lax
from jax.experimental import pallas as pl
from jax.experimental.pallas import tpu as pltpu
from jax.sharding import PartitionSpec as P

negative_fill = -1e30
peak_floor = -1e25
log2_e = 1.4426950408889634
VMEM = pl.BlockSpec(memory_space=pltpu.VMEM)
SMEM = pl.BlockSpec(memory_space=pltpu.SMEM)
HBM = pl.BlockSpec(memory_space=pltpu.HBM)
EXTRA = 16
SLOT, POOL, CORE, TP = range(4)
LARGE = 60


def kernel_params(mib):
    return pltpu.CompilerParams(vmem_limit_bytes=mib * 1024 * 1024)


def cost(flops, moved, exps=0):
    return pl.CostEstimate(flops=flops, bytes_accessed=moved, transcendentals=exps)


def order_kernel(place_ref, trace_ref, cache_ref, out_ref, held, wide, ordered, sems, out_sems):
    traces, rows, size = held.shape
    groups = out_ref.shape[0]
    slots = traces // groups
    copies = [
        pltpu.make_async_copy(cache_ref.at[trace_ref[n]], held.at[n], sems.at[n])
        for n in range(traces)
    ]
    for copy in copies:
        copy.start()
    pending = []
    for n, copy in enumerate(copies):
        copy.wait()
        wide[n % 2] = held[n].astype(jnp.float32)
        for kind in range(2):
            part = wide[n % 2, pl.ds(kind, rows // 2, stride=2), :]
            at = n % slots * rows + kind * (rows // 2)
            ordered[n // slots, pl.ds(at, rows // 2), :] = part.astype(jnp.bfloat16)
        if n % slots == slots - 1:
            group = n // slots
            pending.append(
                pltpu.make_async_copy(ordered.at[group], out_ref.at[group], out_sems.at[group])
            )
            pending[-1].start()
    for copy in pending:
        copy.wait()


def order_blocks(place, slot_trace, prior_rows, groups):
    traces, rows, size = prior_rows.shape
    ordered = (groups, traces // groups * rows, size)
    return pl.pallas_call(
        order_kernel,
        out_shape=jax.ShapeDtypeStruct(ordered, jnp.bfloat16),
        in_specs=[SMEM, SMEM, HBM],
        out_specs=HBM,
        scratch_shapes=[
            pltpu.VMEM((traces, rows, size), jnp.bfloat16),
            pltpu.VMEM((2, rows, size), jnp.float32),
            pltpu.VMEM(ordered, jnp.bfloat16),
            pltpu.SemaphoreType.DMA((traces,)),
            pltpu.SemaphoreType.DMA((groups,)),
        ],
        compiler_params=kernel_params(LARGE),
        cost_estimate=cost(0, 4 * traces * rows * size),
    )(place, slot_trace, prior_rows)


def stage_kernel(
    place_ref, weight_ref, q0, q1, q2, q3, fresh_ref, packed_ref, new_ref, own_ref, *refs
):
    outs, (staged, kept, wide, in_sems, out_sems) = refs[:-5], refs[-5:]
    pools = len(outs) + 1
    size, columns = outs[0].shape
    arriving = []
    for o in range(1, pools):
        to = lax.rem(place_ref[POOL] + pools - o, pools)
        half = weight_ref.at[
            pl.ds(pl.multiple_of(place_ref[CORE] * size, size), size),
            pl.ds(pl.multiple_of(to * columns, columns), columns),
        ]
        arriving.append(pltpu.make_async_copy(half, staged.at[o - 1], in_sems.at[o]))
    own = weight_ref.at[:, pl.ds(pl.multiple_of(place_ref[POOL] * columns, columns), columns)]
    arriving.append(pltpu.make_async_copy(own, kept, in_sems.at[0]))
    for copy in arriving:
        copy.start()
    for n, ref in enumerate((q0, q1, q2, q3)):
        packed_ref[n] = ref[...]
    for slot in range(fresh_ref.shape[0]):
        wide[...] = fresh_ref[slot].astype(jnp.float32)
        for kind in range(2):
            part = wide[pl.ds(kind, wide.shape[0] // 2, stride=2), :]
            new_ref[slot, kind] = part.astype(jnp.bfloat16)
    leaving = [
        pltpu.make_async_copy(source, out, out_sems.at[n])
        for n, (source, out) in enumerate(
            [(staged.at[n], out) for n, out in enumerate(outs)] + [(kept, own_ref)]
        )
    ]
    for n, copy in enumerate(leaving):
        arriving[n].wait()
        copy.start()
    for copy in leaving:
        copy.wait()


def stage(place, weight, queried, fresh):
    pools = len(queried)
    slots, rows, size = fresh.shape
    block = (weight.shape[0] // 2, weight.shape[1] // pools)
    kept = (weight.shape[0], block[1])
    return pl.pallas_call(
        stage_kernel,
        out_shape=[
            jax.ShapeDtypeStruct((pools, *queried[0].shape), jnp.bfloat16),
            jax.ShapeDtypeStruct((slots, 2, rows // 2, size), jnp.bfloat16),
            jax.ShapeDtypeStruct(kept, jnp.bfloat16),
        ]
        + [jax.ShapeDtypeStruct(block, jnp.bfloat16)] * (pools - 1),
        in_specs=[SMEM, HBM] + [VMEM] * (pools + 1),
        out_specs=[VMEM] * 2 + [HBM] * pools,
        scratch_shapes=[
            pltpu.VMEM((pools - 1, *block), jnp.bfloat16),
            pltpu.VMEM(kept, jnp.bfloat16),
            pltpu.VMEM((rows, size), jnp.float32),
            pltpu.SemaphoreType.DMA((pools,)),
            pltpu.SemaphoreType.DMA((pools,)),
        ],
        compiler_params=kernel_params(LARGE),
        cost_estimate=cost(0, 8 * pools * block[0] * block[1]),
    )(place, weight, *queried, fresh)


def attend_kernel(
    place_ref, trace_ref, length_ref, query_ref, new_ref, prior_ref, pay_ref
):
    pools, slots, rows, size = query_ref.shape
    sources, block = prior_ref.shape[0], prior_ref.shape[1] // (2 * slots)
    width = sources * block
    factor = size**-0.5 * log2_e
    contract = (((1,), (1,)), ((), ()))
    position = lax.broadcasted_iota(jnp.int32, (1, width), 1)
    for slot in range(slots):
        valid = length_ref[trace_ref[place_ref[SLOT] + slot]] - place_ref[POOL] * width
        usable = position < valid
        at = 2 * slot * block
        keys = prior_ref[:, pl.ds(at, block), :].reshape(width, size)
        values = prior_ref[:, pl.ds(at + block, block), :].reshape(width, size)
        for tile in range(pools):
            pay = pay_ref.at[lax.rem(place_ref[POOL] + tile, pools)]
            query = query_ref[tile, slot]
            scores = lax.dot_general(query, keys, contract, preferred_element_type=jnp.float32)
            scores = jnp.where(usable, scores, negative_fill)
            peak = jnp.max(scores, -1, keepdims=True)
            if tile == 0:
                fresh_scores = lax.dot_general(
                    query, new_ref[slot, 0], contract, preferred_element_type=jnp.float32
                )
                heads = rows // fresh_scores.shape[1]
                token = lax.broadcasted_iota(jnp.int32, fresh_scores.shape, 0) // heads
                causal = lax.broadcasted_iota(jnp.int32, fresh_scores.shape, 1) <= token
                fresh_scores = jnp.where(causal, fresh_scores, negative_fill)
                peak = jnp.maximum(peak, jnp.max(fresh_scores, -1, keepdims=True))
            peak = jnp.maximum(peak * factor, peak_floor).astype(jnp.bfloat16).astype(jnp.float32)
            weights = jnp.exp2(scores * factor - peak)
            total = jnp.sum(weights, -1, keepdims=True)
            blended = jnp.dot(
                weights.astype(jnp.bfloat16), values, preferred_element_type=jnp.float32
            )
            if tile == 0:
                fresh_weights = jnp.exp2(fresh_scores * factor - peak)
                total = total + jnp.sum(fresh_weights, -1, keepdims=True)
                blended = blended + jnp.dot(
                    fresh_weights.astype(jnp.bfloat16),
                    new_ref[slot, 1],
                    preferred_element_type=jnp.float32,
                )
            pay[pl.ds(slot * rows, rows), :] = blended.astype(jnp.bfloat16)
            high = total.astype(jnp.bfloat16).astype(jnp.float32)
            columns = columns_of((rows, size), (peak, high, total - high))
            halves = [columns[n : n + size].T[:8] for n in range(0, rows, size)]
            pay[pl.ds(slots * rows + slot * EXTRA, EXTRA), :] = jnp.concatenate(halves, 0).astype(
                jnp.bfloat16
            )


def attend(place, slot_trace, prefix_length, queries, new, prior):
    pools, slots, rows, size = queries.shape
    width = prior.shape[0] * prior.shape[1] // (2 * slots)
    return pl.pallas_call(
        attend_kernel,
        out_shape=jax.ShapeDtypeStruct((pools, slots * (rows + EXTRA), size), jnp.bfloat16),
        in_specs=[SMEM] * 3 + [VMEM] * 3,
        out_specs=VMEM,
        compiler_params=kernel_params(24),
        cost_estimate=cost(32 * rows * width * size, 8 * width * size, 8 * rows * width),
    )(place, slot_trace, prefix_length, queries, new, prior)


def columns_of(shape, columns):
    lane = lax.broadcasted_iota(jnp.int32, shape, 1)
    laid = jnp.zeros(shape, jnp.float32)
    for n, column in enumerate(columns):
        laid = jnp.where(lane == n, column, laid)
    return laid


def rows_of(shape, rows):
    at = lax.broadcasted_iota(jnp.int32, shape, 0)
    laid = jnp.zeros(shape, jnp.float32)
    for n, row in enumerate(rows):
        laid = jnp.where(at == n, row, laid)
    return laid


def split_three(value):
    high = value.astype(jnp.bfloat16).astype(jnp.float32)
    middle = (value - high).astype(jnp.bfloat16).astype(jnp.float32)
    return high, middle, value - high - middle


def merge_kernel(pay_ref, out_ref, wide):
    rows, size = wide.shape
    heads = rows // size
    pools = out_ref.shape[0]
    slots = out_ref.shape[1] // rows
    for slot in range(slots):
        peaks, totals = [], []
        for n in range(pools):
            stats = pay_ref[n, pl.ds(slots * rows + slot * EXTRA, EXTRA), :].astype(jnp.float32)
            columns = jnp.concatenate(
                [
                    jnp.concatenate([stats[8 * half : 8 * half + 8]] * (size // 8), 0).T
                    for half in range(heads)
                ],
                0,
            )
            peaks.append(columns[:, 0:1])
            totals.append(columns[:, 1:2] + columns[:, 2:3])
        top = functools.reduce(jnp.maximum, peaks)
        shares = [jnp.exp2(peak - top) for peak in peaks]
        total = sum(share * part for share, part in zip(shares, totals))
        blended = sum(
            share * pay_ref[n, pl.ds(slot * rows, rows), :].astype(jnp.float32)
            for n, share in enumerate(shares)
        )
        wide[...] = blended / total
        for head in range(heads):
            part = wide[pl.ds(head, size, stride=heads), :].astype(jnp.bfloat16)
            for n in range(pools):
                out_ref[n, pl.ds(slot * rows + head * size, size), :] = part


def merge(pays, slots):
    pools, rows, size = pays.shape
    rows = rows // slots - EXTRA
    return pl.pallas_call(
        merge_kernel,
        out_shape=jax.ShapeDtypeStruct((pools, slots * rows, size), jnp.bfloat16),
        in_specs=[VMEM],
        out_specs=VMEM,
        scratch_shapes=[pltpu.VMEM((rows, size), jnp.float32)],
        compiler_params=kernel_params(8),
        cost_estimate=cost(0, 20 * rows * size),
    )(pays)


def project_kernel(place_ref, attended_ref, weight_ref, *refs):
    moved, (out_ref, weights, sems) = refs[:-3], refs[-3:]
    dests, wide = out_ref.shape[0], out_ref.shape[2]
    pools, tokens, size = attended_ref.shape[0], out_ref.shape[1], attended_ref.shape[2]
    slots = tokens // size
    columns = weights.shape[2]
    chunks = sems.shape[0]
    span = columns // chunks
    core = place_ref[CORE]
    copies = []
    for chunk in range(chunks):
        at = pl.ds(chunk * span, span)
        batch = [(weight_ref.at[:, at], weights.at[0, :, at])]
        for n, ref in enumerate(moved):
            half = core if n % 2 == 0 else 1 - core
            rows = pl.ds(pl.multiple_of(half * size, size), size)
            batch.append((ref.at[pl.ds(0, size), at], weights.at[1 + n // 2, rows, at]))
        copies.append([
            pltpu.make_async_copy(source, target, sems.at[chunk, n])
            for n, (source, target) in enumerate(batch)
        ])
        for copy in copies[-1]:
            copy.start()
    inputs = []
    for n in range(pools):
        ref = attended_ref.at[lax.rem(place_ref[POOL] + n, pools)]
        rows = [
            jnp.concatenate([ref[pl.ds(at, size), :], ref[pl.ds(at + size, size), :]], 1)
            for at in range(0, 2 * slots * size, 2 * size)
        ]
        inputs.append(jnp.concatenate(rows, 0))
    for chunk in range(chunks):
        for copy in copies[chunk]:
            copy.wait()
        for dest in range(chunk * dests // chunks, (chunk + 1) * dests // chunks):
            at = pl.ds(dest * wide, wide)
            total = jnp.dot(inputs[0], weights[0, :, at], preferred_element_type=jnp.float32)
            for n in range(1, pools):
                total += jnp.dot(inputs[n], weights[n, :, at], preferred_element_type=jnp.float32)
            out_ref[dest] = total.astype(jnp.bfloat16)


def project(place, attended, weight, moved, dests):
    pools, rows, size = attended.shape
    tokens = rows // 2
    columns = moved[0].shape[1]
    chunks = 4
    return pl.pallas_call(
        project_kernel,
        out_shape=jax.ShapeDtypeStruct((dests, tokens, columns // dests), jnp.bfloat16),
        in_specs=[SMEM, VMEM] + [HBM] * (1 + len(moved)),
        out_specs=VMEM,
        scratch_shapes=[
            pltpu.VMEM((pools, weight.shape[0], columns), jnp.bfloat16),
            pltpu.SemaphoreType.DMA((chunks, 1 + len(moved))),
        ],
        compiler_params=kernel_params(16),
        cost_estimate=cost(16 * tokens * size * columns, 16 * size * columns),
    )(place, attended, weight, *moved)


def finish_kernel(arrived_ref, bound_ref, reward_ref, out_ref, spread_ref):
    slots, tokens, wide = out_ref.shape
    steps = bound_ref.shape[1]
    for slot in range(slots):
        total = jnp.zeros((tokens, wide), jnp.float32)
        for n in range(arrived_ref.shape[0]):
            total += arrived_ref[n, pl.ds(slot * tokens, tokens), :].astype(jnp.float32)
        out_ref[slot] = total.astype(jnp.bfloat16)
        rounded = out_ref[slot].astype(jnp.float32)
        row = jnp.sum(rounded * reward_ref[...], -1, keepdims=True)
        lane = lax.broadcasted_iota(jnp.int32, (tokens, steps), 0)
        chosen = jnp.sum(jnp.where(lane == bound_ref[slot : slot + 1, :], row, 0.0), 0, keepdims=True)
        for n in range(spread_ref.shape[0]):
            spread_ref[n, slot : slot + 1, :] = chosen


def finish(arrived, boundaries, reward, spread):
    slots, steps = boundaries.shape
    _, rows, wide = arrived.shape
    return pl.pallas_call(
        finish_kernel,
        out_shape=[
            jax.ShapeDtypeStruct((slots, rows // slots, wide), jnp.bfloat16),
            jax.ShapeDtypeStruct((spread, slots, steps), jnp.float32),
        ],
        in_specs=[VMEM] * 3,
        out_specs=[VMEM] * 2,
        compiler_params=kernel_params(8),
    )(arrived, boundaries, reward)


def shards(
    prior_cache,
    prefix_length,
    slot_trace,
    queries,
    new_token_cache,
    boundaries,
    output_weight,
    reward_weight,
):
    pool, seq, tp = lax.axis_index("pool"), lax.axis_index("seq"), lax.axis_index("tp")
    pools, seqs, tps = lax.axis_size("pool"), lax.axis_size("seq"), lax.axis_size("tp")
    slots, new_len, _, pair, size = queries.shape
    traces, block = prior_cache.shape[:2]
    place = jnp.stack([seq * slots, pool, lax.rem(seq, 2), tp]).astype(jnp.int32)
    rows_all = output_weight.reshape(pair * size, -1)
    prior_rows = prior_cache.reshape(traces, 2 * block, size)
    own_queries = queries.reshape(slots, new_len * pair, size)

    def from_pool(array, offset):
        return lax.ppermute(array, "pool", [((n + offset) % pools, n) for n in range(pools)])

    def turn(array, axes):
        return lax.all_to_all(array, axes, split_axis=0, concat_axis=0, tiled=True)

    def swap_core(array):
        return lax.ppermute(array, "seq", [(n, n ^ 1) for n in range(seqs)])

    sent = order_blocks(place, slot_trace, prior_rows, seqs)
    sent, own_queries = lax.optimization_barrier((sent, own_queries))
    prior = turn(sent, "seq")

    queried = [own_queries] + [from_pool(own_queries, o) for o in range(1, pools)]
    fresh = new_token_cache.reshape(slots, 2 * new_len, size)
    packed, new, kept, *leaving = stage(place, rows_all, queried, fresh)
    came = [from_pool(part, o) for o, part in enumerate(leaving, 1)]
    pays = attend(place, slot_trace, prefix_length, packed, new, prior)
    pays, came = lax.optimization_barrier((turn(pays, "pool"), came))
    moved = [part for got in came for part in (got, swap_core(got))]
    gathered = turn(merge(pays, slots), "pool")
    partial = project(place, gathered, kept, moved, tps)
    arrived = turn(partial, "tp")
    layer_out, spread = finish(arrived, boundaries, reward_weight.reshape(1, -1), pools * tps)
    return (layer_out, jnp.sum(turn(spread, ("pool", "tp")), 0))


def solution(mesh):
    placed = (
        P(None, ("pool", "seq"), "tp", None, None),
        P(),
        P(),
        P("seq", None, "tp", "pool", None),
        P("seq", None, "tp", None, None),
        P("seq", None),
        P("tp", "pool", None, None),
        P(("pool", "tp")),
    )
    return jax.shard_map(
        shards,
        mesh=mesh,
        in_specs=placed,
        out_specs=(P("seq", None, ("pool", "tp")), P("seq", None)),
        check_vma=False,
    )
```

```python
import functools

import jax
import jax.numpy as jnp
from jax import lax
from jax.experimental import pallas as pl
from jax.experimental.pallas import tpu as pltpu
from jax.sharding import PartitionSpec as P

negative_fill = -1e30
peak_floor = -1e25
log2_e = 1.4426950408889634
VMEM = pl.BlockSpec(memory_space=pltpu.VMEM)
SMEM = pl.BlockSpec(memory_space=pltpu.SMEM)
HBM = pl.BlockSpec(memory_space=pltpu.HBM)
EXTRA = 16
SLOT, POOL, CORE, TP = range(4)
LARGE = 60


def kernel_params(mib):
    return pltpu.CompilerParams(vmem_limit_bytes=mib * 1024 * 1024)


def cost(flops, moved, exps=0):
    return pl.CostEstimate(flops=flops, bytes_accessed=moved, transcendentals=exps)


def order_kernel(
    place_ref, trace_ref, cache_ref, query_ref, reward_ref, out_ref, leaving_ref,
    held, wide, ordered, laid, sems, out_sems, own_sems,
):
    traces, rows, size = held.shape
    groups = out_ref.shape[0]
    slots = traces // groups
    copies = [
        pltpu.make_async_copy(cache_ref.at[trace_ref[n]], held.at[n], sems.at[n])
        for n in range(traces)
    ]
    for copy in copies:
        copy.start()
    query_rows = query_ref.shape[0]
    query_copy = pltpu.make_async_copy(query_ref, laid.at[pl.ds(0, query_rows), :], own_sems.at[0])
    query_copy.start()
    pieces = split_three(reward_ref[...])
    pieces = [piece[half : half + 1, :] for half in range(2) for piece in pieces]
    laid[pl.ds(query_rows, EXTRA), :] = rows_of((EXTRA, size), pieces).astype(jnp.bfloat16)
    pending = []
    for n, copy in enumerate(copies):
        copy.wait()
        wide[n % 2] = held[n].astype(jnp.float32)
        for kind in range(2):
            part = wide[n % 2, pl.ds(kind, rows // 2, stride=2), :]
            at = n % slots * rows + kind * (rows // 2)
            ordered[n // slots, pl.ds(at, rows // 2), :] = part.astype(jnp.bfloat16)
        if n % slots == slots - 1:
            group = n // slots
            pending.append(
                pltpu.make_async_copy(ordered.at[group], out_ref.at[group], out_sems.at[group])
            )
            pending[-1].start()
        if n == traces // 2:
            query_copy.wait()
            pending.append(pltpu.make_async_copy(laid, leaving_ref, own_sems.at[1]))
            pending[-1].start()
    for copy in pending:
        copy.wait()


def order_blocks(place, slot_trace, prior_rows, queries, reward, groups):
    traces, rows, size = prior_rows.shape
    ordered = (groups, traces // groups * rows, size)
    laid = (queries.shape[0] + EXTRA, size)
    return pl.pallas_call(
        order_kernel,
        out_shape=[
            jax.ShapeDtypeStruct(ordered, jnp.bfloat16),
            jax.ShapeDtypeStruct(laid, jnp.bfloat16),
        ],
        in_specs=[SMEM, SMEM, HBM, HBM, VMEM],
        out_specs=[HBM, HBM],
        scratch_shapes=[
            pltpu.VMEM((traces, rows, size), jnp.bfloat16),
            pltpu.VMEM((2, rows, size), jnp.float32),
            pltpu.VMEM(ordered, jnp.bfloat16),
            pltpu.VMEM(laid, jnp.bfloat16),
            pltpu.SemaphoreType.DMA((traces,)),
            pltpu.SemaphoreType.DMA((groups,)),
            pltpu.SemaphoreType.DMA((2,)),
        ],
        compiler_params=kernel_params(LARGE),
        cost_estimate=cost(0, 4 * traces * rows * size),
    )(place, slot_trace, prior_rows, queries, reward)


def stage_kernel(place_ref, weight_ref, *refs):
    outs, (staged, kept, in_sems, out_sems) = refs[-8:-4], refs[-4:]
    pools = len(outs)
    size, columns = outs[0].shape
    arriving = []
    for o in range(1, pools):
        to = lax.rem(place_ref[POOL] + pools - o, pools)
        half = weight_ref.at[
            pl.ds(pl.multiple_of(place_ref[CORE] * size, size), size),
            pl.ds(pl.multiple_of(to * columns, columns), columns),
        ]
        arriving.append(pltpu.make_async_copy(half, staged.at[o - 1], in_sems.at[o]))
    own = weight_ref.at[:, pl.ds(pl.multiple_of(place_ref[POOL] * columns, columns), columns)]
    arriving.append(pltpu.make_async_copy(own, kept, in_sems.at[0]))
    for copy in arriving:
        copy.start()
    sources = [staged.at[n] for n in range(pools - 1)] + [kept]
    leaving = [
        pltpu.make_async_copy(source, out, out_sems.at[n])
        for n, (source, out) in enumerate(zip(sources, outs))
    ]
    for n, copy in enumerate(leaving):
        arriving[n].wait()
        copy.start()
    for copy in leaving:
        copy.wait()


def stage(place, weight, pools, behind):
    block = (weight.shape[0] // 2, weight.shape[1] // pools)
    kept = (weight.shape[0], block[1])
    return pl.pallas_call(
        stage_kernel,
        out_shape=[jax.ShapeDtypeStruct(block, jnp.bfloat16)] * (pools - 1)
        + [jax.ShapeDtypeStruct(kept, jnp.bfloat16)],
        in_specs=[SMEM, HBM, HBM],
        out_specs=[HBM] * pools,
        scratch_shapes=[
            pltpu.VMEM((pools - 1, *block), jnp.bfloat16),
            pltpu.VMEM(kept, jnp.bfloat16),
            pltpu.SemaphoreType.DMA((pools,)),
            pltpu.SemaphoreType.DMA((pools,)),
        ],
        compiler_params=kernel_params(LARGE),
        cost_estimate=cost(0, 8 * pools * block[0] * block[1]),
    )(place, weight, behind)


def pack_kernel(
    place_ref, q0, q1, q2, q3, fresh_ref, behind_ref, packed_ref, new_ref, head_ref, wide
):
    slots, rows = packed_ref.shape[1:3]
    head_ref[...] = jnp.zeros_like(head_ref)
    found = []
    for n, ref in enumerate((q0, q1, q2, q3)):
        for slot in range(slots):
            packed_ref[n, slot] = ref[pl.ds(slot * rows, rows), :]
        pieces = ref[pl.ds(slots * rows, EXTRA), :].astype(jnp.float32)
        found += [three_rows(pieces, half) for half in range(2)]
    count = len(found)
    at = pl.ds(pl.multiple_of(place_ref[TP] * count, count), count)
    head_ref[at, :] = rows_of((count, wide.shape[1]), found)
    for slot in range(slots):
        wide[...] = fresh_ref[slot].astype(jnp.float32)
        for kind in range(2):
            part = wide[pl.ds(kind, wide.shape[0] // 2, stride=2), :]
            new_ref[slot, kind] = part.astype(jnp.bfloat16)


def pack(place, queried, fresh, behind, tps):
    pools = len(queried)
    slots, rows, size = fresh.shape
    per_slot = (queried[0].shape[0] - EXTRA) // slots
    return pl.pallas_call(
        pack_kernel,
        out_shape=[
            jax.ShapeDtypeStruct((pools, slots, per_slot, size), jnp.bfloat16),
            jax.ShapeDtypeStruct((slots, 2, rows // 2, size), jnp.bfloat16),
            jax.ShapeDtypeStruct((tps * pools * 2, size), jnp.float32),
        ],
        in_specs=[SMEM] + [VMEM] * (pools + 1) + [HBM],
        out_specs=[VMEM] * 3,
        scratch_shapes=[pltpu.VMEM((rows, size), jnp.float32)],
        compiler_params=kernel_params(8),
        cost_estimate=cost(0, 4 * pools * slots * per_slot * size),
    )(place, *queried, fresh, behind)


def reward_rows_kernel(place_ref, weight_ref, head_ref, out_ref, weights, sems):
    pools, rows, columns = weights.shape
    size = out_ref.shape[1]
    copies = []
    for n in range(pools):
        start = pl.multiple_of(lax.rem(place_ref[POOL] + n, pools) * columns, columns)
        copies.append(
            pltpu.make_async_copy(weight_ref.at[:, pl.ds(start, columns)], weights.at[n], sems.at[n])
        )
        copies[-1].start()
    total = jnp.zeros((rows, size), jnp.float32)
    for n, copy in enumerate(copies):
        copy.wait()
        for m in range(columns // size):
            at = 2 * (m // 2 * pools + n) + m % 2
            part = weights[n, :, pl.ds(m * size, size)].astype(jnp.float32)
            total += part * head_ref[at : at + 1, :]
    column = jnp.sum(total, -1, keepdims=True)
    for n in range(rows // size):
        row = jnp.broadcast_to(column[n * size : (n + 1) * size], (size, size)).T
        out_ref[pl.ds(4 * n, 4), :] = row[:4]


def reward_rows(place, weight_rows, head, pools):
    rows, columns = weight_rows.shape
    size = head.shape[1]
    return pl.pallas_call(
        reward_rows_kernel,
        out_shape=jax.ShapeDtypeStruct((4 * rows // size, size), jnp.float32),
        in_specs=[SMEM, HBM, VMEM],
        out_specs=VMEM,
        scratch_shapes=[
            pltpu.VMEM((pools, rows, columns // pools), jnp.bfloat16),
            pltpu.SemaphoreType.DMA((pools,)),
        ],
        compiler_params=kernel_params(LARGE),
        cost_estimate=cost(16 * rows * columns, 2 * rows * columns),
    )(place, weight_rows, head)


def attend_kernel(
    place_ref, trace_ref, length_ref, query_ref, new_ref, behind_ref, prior_ref, pay_ref
):
    pools, slots, rows, size = query_ref.shape
    sources, block = prior_ref.shape[0], prior_ref.shape[1] // (2 * slots)
    width = sources * block
    factor = size**-0.5 * log2_e
    contract = (((1,), (1,)), ((), ()))
    position = lax.broadcasted_iota(jnp.int32, (1, width), 1)

    def keys_of(slot):
        return prior_ref[:, pl.ds(2 * slot * block, block), :].reshape(width, size)

    def scores_of(slot, tile):
        return lax.dot_general(
            query_ref[tile, slot], keys_of(slot), contract, preferred_element_type=jnp.float32
        )

    ahead = scores_of(0, 0)
    for slot in range(slots):
        valid = length_ref[trace_ref[place_ref[SLOT] + slot]] - place_ref[POOL] * width
        usable = position < valid
        values = prior_ref[:, pl.ds((2 * slot + 1) * block, block), :].reshape(width, size)
        for tile in range(pools):
            pay = pay_ref.at[lax.rem(place_ref[POOL] + tile, pools)]
            query = query_ref[tile, slot]
            scores = ahead
            if tile < pools - 1:
                ahead = scores_of(slot, tile + 1)
            elif slot < slots - 1:
                ahead = scores_of(slot + 1, 0)
            scores = jnp.where(usable, scores, negative_fill)
            peak = jnp.max(scores, -1, keepdims=True)
            if tile == 0:
                fresh_scores = lax.dot_general(
                    query, new_ref[slot, 0], contract, preferred_element_type=jnp.float32
                )
                heads = rows // fresh_scores.shape[1]
                token = lax.broadcasted_iota(jnp.int32, fresh_scores.shape, 0) // heads
                causal = lax.broadcasted_iota(jnp.int32, fresh_scores.shape, 1) <= token
                fresh_scores = jnp.where(causal, fresh_scores, negative_fill)
                peak = jnp.maximum(peak, jnp.max(fresh_scores, -1, keepdims=True))
            peak = jnp.maximum(peak * factor, peak_floor).astype(jnp.bfloat16).astype(jnp.float32)
            weights = jnp.exp2(scores * factor - peak)
            total = jnp.sum(weights, -1, keepdims=True)
            blended = jnp.dot(
                weights.astype(jnp.bfloat16), values, preferred_element_type=jnp.float32
            )
            if tile == 0:
                fresh_weights = jnp.exp2(fresh_scores * factor - peak)
                total = total + jnp.sum(fresh_weights, -1, keepdims=True)
                blended = blended + jnp.dot(
                    fresh_weights.astype(jnp.bfloat16),
                    new_ref[slot, 1],
                    preferred_element_type=jnp.float32,
                )
            pay[pl.ds(slot * rows, rows), :] = blended.astype(jnp.bfloat16)
            high = total.astype(jnp.bfloat16).astype(jnp.float32)
            columns = columns_of((rows, size), (peak, high, total - high))
            halves = [columns[n : n + size].T[:8] for n in range(0, rows, size)]
            pay[pl.ds(slots * rows + slot * EXTRA, EXTRA), :] = jnp.concatenate(halves, 0).astype(
                jnp.bfloat16
            )


def attend(place, slot_trace, prefix_length, queries, new, behind, prior):
    pools, slots, rows, size = queries.shape
    width = prior.shape[0] * prior.shape[1] // (2 * slots)
    return pl.pallas_call(
        attend_kernel,
        out_shape=jax.ShapeDtypeStruct((pools, slots * (rows + EXTRA), size), jnp.bfloat16),
        in_specs=[SMEM] * 3 + [VMEM] * 4,
        out_specs=VMEM,
        compiler_params=kernel_params(24),
        cost_estimate=cost(32 * rows * width * size, 8 * width * size, 8 * rows * width),
    )(place, slot_trace, prefix_length, queries, new, behind, prior)


def columns_of(shape, columns):
    lane = lax.broadcasted_iota(jnp.int32, shape, 1)
    laid = jnp.zeros(shape, jnp.float32)
    for n, column in enumerate(columns):
        laid = jnp.where(lane == n, column, laid)
    return laid


def rows_of(shape, rows):
    at = lax.broadcasted_iota(jnp.int32, shape, 0)
    laid = jnp.zeros(shape, jnp.float32)
    for n, row in enumerate(rows):
        laid = jnp.where(at == n, row, laid)
    return laid


def split_three(value):
    high = value.astype(jnp.bfloat16).astype(jnp.float32)
    middle = (value - high).astype(jnp.bfloat16).astype(jnp.float32)
    return high, middle, value - high - middle


def merge_kernel(pay_ref, seen_ref, out_ref, wide):
    rows, size = wide.shape
    heads = rows // size
    pools = out_ref.shape[0]
    slots = out_ref.shape[1] // rows
    for slot in range(slots):
        peaks, totals = [], []
        for n in range(pools):
            stats = pay_ref[n, pl.ds(slots * rows + slot * EXTRA, EXTRA), :].astype(jnp.float32)
            laid = jnp.concatenate(
                [
                    jnp.concatenate([stats[8 * half : 8 * half + 8]] * (size // 8), 0).T
                    for half in range(heads)
                ],
                0,
            )
            peaks.append(laid[:, 0:1])
            totals.append(laid[:, 1:2] + laid[:, 2:3])
        top = functools.reduce(jnp.maximum, peaks)
        shares = [jnp.exp2(peak - top) for peak in peaks]
        total = sum(share * part for share, part in zip(shares, totals))
        blended = sum(
            share * pay_ref[n, pl.ds(slot * rows, rows), :].astype(jnp.float32)
            for n, share in enumerate(shares)
        )
        wide[...] = blended / total
        for head in range(heads):
            part = wide[pl.ds(head, size, stride=heads), :].astype(jnp.bfloat16)
            for n in range(pools):
                out_ref[n, pl.ds(slot * rows + head * size, size), :] = part
    rewards = []
    for slot in range(slots):
        reward = jnp.zeros((size, 1), jnp.float32)
        for head in range(heads):
            part = out_ref[0, pl.ds(slot * rows + head * size, size), :].astype(jnp.float32)
            reward += jnp.sum(part * seen_ref[4 * head : 4 * head + 1, :], -1, keepdims=True)
        rewards += split_three(reward)
    laid = columns_of((size, size), rewards).T[:EXTRA].astype(jnp.bfloat16)
    for n in range(pools):
        out_ref[n, pl.ds(slots * rows, EXTRA), :] = laid


def merge(pays, seen, slots):
    pools, rows, size = pays.shape
    rows = rows // slots - EXTRA
    return pl.pallas_call(
        merge_kernel,
        out_shape=jax.ShapeDtypeStruct((pools, slots * rows + EXTRA, size), jnp.bfloat16),
        in_specs=[VMEM] * 2,
        out_specs=VMEM,
        scratch_shapes=[pltpu.VMEM((rows, size), jnp.float32)],
        compiler_params=kernel_params(8),
        cost_estimate=cost(0, 20 * rows * size),
    )(pays, seen)


def project_kernel(place_ref, attended_ref, weight_ref, *refs):
    outs, (weights, sems) = refs[-10:-2], refs[-2:]
    moved, dests, wide = refs[:-10], len(outs), outs[0].shape[1]
    pools, tokens, size = attended_ref.shape[0], outs[0].shape[0] - EXTRA, attended_ref.shape[2]
    slots = tokens // size
    columns = weights.shape[2]
    chunks = sems.shape[0]
    span = columns // chunks
    core = place_ref[CORE]
    copies = []
    for chunk in range(chunks):
        at = pl.ds(chunk * span, span)
        batch = [(weight_ref.at[:, at], weights.at[0, :, at])]
        for n, ref in enumerate(moved):
            half = core if n % 2 == 0 else 1 - core
            rows = pl.ds(pl.multiple_of(half * size, size), size)
            batch.append((ref.at[pl.ds(0, size), at], weights.at[1 + n // 2, rows, at]))
        copies.append([
            pltpu.make_async_copy(source, target, sems.at[chunk, n])
            for n, (source, target) in enumerate(batch)
        ])
        for copy in copies[-1]:
            copy.start()
    inputs = []
    for n in range(pools):
        ref = attended_ref.at[lax.rem(place_ref[POOL] + n, pools)]
        rows = [
            jnp.concatenate([ref[pl.ds(at, size), :], ref[pl.ds(at + size, size), :]], 1)
            for at in range(0, 2 * slots * size, 2 * size)
        ]
        inputs.append(jnp.concatenate(rows, 0))
    rewards = jnp.zeros((EXTRA, size), jnp.float32)
    for n in range(pools):
        rewards += attended_ref[n, pl.ds(2 * tokens, EXTRA), :].astype(jnp.float32)
    pieces = []
    for slot in range(slots):
        pieces += split_three(three_rows(rewards, slot))
    laid = rows_of((EXTRA, size), pieces)
    laid = jnp.concatenate([laid, jnp.zeros_like(laid)], 1).astype(jnp.bfloat16)
    for out in outs:
        out[pl.ds(tokens, EXTRA), :] = laid
    for chunk in range(chunks):
        for copy in copies[chunk]:
            copy.wait()
    for o, out in enumerate(outs):
        dest = lax.rem(place_ref[TP] + o, dests)
        at = pl.ds(pl.multiple_of(dest * wide, wide), wide)
        total = jnp.dot(inputs[0], weights[0, :, at], preferred_element_type=jnp.float32)
        for n in range(1, pools):
            total += jnp.dot(inputs[n], weights[n, :, at], preferred_element_type=jnp.float32)
        out[pl.ds(0, tokens), :] = total.astype(jnp.bfloat16)


def project(place, attended, weight, moved, dests):
    pools, rows, size = attended.shape
    tokens = (rows - EXTRA) // 2
    columns = moved[0].shape[1]
    chunks = 1
    return pl.pallas_call(
        project_kernel,
        out_shape=[jax.ShapeDtypeStruct((tokens + EXTRA, columns // dests), jnp.bfloat16)] * dests,
        in_specs=[SMEM, VMEM] + [HBM] * (1 + len(moved)),
        out_specs=[VMEM] * dests,
        scratch_shapes=[
            pltpu.VMEM((pools, weight.shape[0], columns), jnp.bfloat16),
            pltpu.SemaphoreType.DMA((chunks, 1 + len(moved))),
        ],
        compiler_params=kernel_params(16),
        cost_estimate=cost(16 * tokens * size * columns, 16 * size * columns),
    )(place, attended, weight, *moved)


def three_rows(array, slot):
    return sum(array[3 * slot + n : 3 * slot + n + 1] for n in range(3))


def finish_kernel(*refs):
    arrived, (bound_ref, out_ref, reward_ref) = refs[:-3], refs[-3:]
    slots, tokens, wide = out_ref.shape
    steps = bound_ref.shape[1]
    rewards = jnp.zeros((EXTRA, wide), jnp.float32)
    for ref in arrived:
        rewards += ref[pl.ds(slots * tokens, EXTRA), :].astype(jnp.float32)
    for slot in range(slots):
        total = jnp.zeros((tokens, wide), jnp.float32)
        for ref in arrived:
            total += ref[pl.ds(slot * tokens, tokens), :].astype(jnp.float32)
        out_ref[slot] = total.astype(jnp.bfloat16)
        row = jnp.broadcast_to(three_rows(rewards, slot)[:, :tokens], (tokens, tokens)).T[:, :steps]
        lane = lax.broadcasted_iota(jnp.int32, (tokens, steps), 0)
        chosen = jnp.where(lane == bound_ref[slot : slot + 1, :], row, 0.0)
        reward_ref[slot : slot + 1, :] = jnp.sum(chosen, 0, keepdims=True)


def finish(arrived, boundaries):
    slots, steps = boundaries.shape
    rows, wide = arrived[0].shape
    return pl.pallas_call(
        finish_kernel,
        out_shape=[
            jax.ShapeDtypeStruct((slots, (rows - EXTRA) // slots, wide), jnp.bfloat16),
            jax.ShapeDtypeStruct((slots, steps), jnp.float32),
        ],
        in_specs=[VMEM] * (1 + len(arrived)),
        out_specs=[VMEM] * 2,
        compiler_params=kernel_params(8),
    )(*arrived, boundaries)


def shards(
    prior_cache,
    prefix_length,
    slot_trace,
    queries,
    new_token_cache,
    boundaries,
    output_weight,
    reward_weight,
):
    pool, seq, tp = lax.axis_index("pool"), lax.axis_index("seq"), lax.axis_index("tp")
    pools, seqs, tps = lax.axis_size("pool"), lax.axis_size("seq"), lax.axis_size("tp")
    slots, new_len, _, pair, size = queries.shape
    traces, block = prior_cache.shape[:2]
    place = jnp.stack([seq * slots, pool, lax.rem(seq, 2), tp]).astype(jnp.int32)
    rows_all = output_weight.reshape(pair * size, -1)
    prior_rows = prior_cache.reshape(traces, 2 * block, size)
    own_queries = queries.reshape(slots * new_len * pair, size)

    def from_pool(array, offset):
        return lax.ppermute(array, "pool", [((n + offset) % pools, n) for n in range(pools)])

    def turn(array, axes):
        return lax.all_to_all(array, axes, split_axis=0, concat_axis=0, tiled=True)

    def swap_core(array):
        return lax.ppermute(array, "seq", [(n, n ^ 1) for n in range(seqs)])

    sent, own = order_blocks(
        place, slot_trace, prior_rows, own_queries, reward_weight.reshape(-1, size), seqs
    )
    prior = turn(sent, "seq")

    queried = [own] + [from_pool(own, o) for o in range(1, pools)]
    *leaving, kept = stage(place, rows_all, pools, own)
    came = [from_pool(part, o) for o, part in enumerate(leaving, 1)]
    fresh = new_token_cache.reshape(slots, 2 * new_len, size)
    packed, new, head = pack(place, queried, fresh, kept, tps)

    step = 1
    while step < tps:
        head = head + lax.ppermute(head, "tp", [(n, n ^ step) for n in range(tps)])
        step *= 2
    seen = reward_rows(place, rows_all, head, pools)

    pays = attend(place, slot_trace, prefix_length, packed, new, seen, prior)
    pays, came = lax.optimization_barrier((turn(pays, "pool"), came))
    moved = [part for got in came for part in (got, swap_core(got))]
    gathered = turn(merge(pays, seen, slots), "pool")
    partial = project(place, gathered, kept, moved, tps)
    arrived = [partial[0]] + [
        lax.ppermute(partial[o], "tp", [(n, (n + o) % tps) for n in range(tps)])
        for o in (4, 3, 5, 2, 6, 1, 7)
    ]
    return tuple(finish(arrived, boundaries))


def solution(mesh):
    placed = (
        P(None, ("pool", "seq"), "tp", None, None),
        P(),
        P(),
        P("seq", None, "tp", "pool", None),
        P("seq", None, "tp", None, None),
        P("seq", None),
        P("tp", "pool", None, None),
        P(("pool", "tp")),
    )
    return jax.shard_map(
        shards,
        mesh=mesh,
        in_specs=placed,
        out_specs=(P("seq", None, ("pool", "tp")), P("seq", None)),
        check_vma=False,
    )
```

```python
import functools

import jax
import jax.numpy as jnp
from jax import lax
from jax.experimental import pallas as pl
from jax.experimental.pallas import tpu as pltpu
from jax.sharding import PartitionSpec as P

negative_fill = -1e30
peak_floor = -1e25
log2_e = 1.4426950408889634
VMEM = pl.BlockSpec(memory_space=pltpu.VMEM)
SMEM = pl.BlockSpec(memory_space=pltpu.SMEM)
HBM = pl.BlockSpec(memory_space=pltpu.HBM)
EXTRA = 16
SLOT, POOL, CORE, TP = range(4)
LARGE = 60


def kernel_params(mib):
    return pltpu.CompilerParams(vmem_limit_bytes=mib * 1024 * 1024)


def cost(flops, moved, exps=0):
    return pl.CostEstimate(flops=flops, bytes_accessed=moved, transcendentals=exps)


def order_kernel(
    place_ref, trace_ref, cache_ref, query_ref, reward_ref, out_ref, leaving_ref,
    held, wide, ordered, laid, sems, out_sems, own_sems,
):
    traces, rows, size = held.shape
    groups = out_ref.shape[0]
    slots = traces // groups
    copies = [
        pltpu.make_async_copy(cache_ref.at[trace_ref[n]], held.at[n], sems.at[n])
        for n in range(traces)
    ]
    for copy in copies:
        copy.start()
    query_rows = query_ref.shape[0]
    query_copy = pltpu.make_async_copy(query_ref, laid.at[pl.ds(0, query_rows), :], own_sems.at[0])
    query_copy.start()
    pieces = split_three(reward_ref[...])
    pieces = [piece[half : half + 1, :] for half in range(2) for piece in pieces]
    laid[pl.ds(query_rows, EXTRA), :] = rows_of((EXTRA, size), pieces).astype(jnp.bfloat16)
    pending = []
    for n, copy in enumerate(copies):
        copy.wait()
        wide[n % 2] = held[n].astype(jnp.float32)
        for kind in range(2):
            part = wide[n % 2, pl.ds(kind, rows // 2, stride=2), :]
            at = n % slots * rows + kind * (rows // 2)
            ordered[n // slots, pl.ds(at, rows // 2), :] = part.astype(jnp.bfloat16)
        if n % slots == slots - 1:
            group = n // slots
            pending.append(
                pltpu.make_async_copy(ordered.at[group], out_ref.at[group], out_sems.at[group])
            )
            pending[-1].start()
        if n == traces // 2:
            query_copy.wait()
            pending.append(pltpu.make_async_copy(laid, leaving_ref, own_sems.at[1]))
            pending[-1].start()
    for copy in pending:
        copy.wait()


def order_blocks(place, slot_trace, prior_rows, queries, reward, groups):
    traces, rows, size = prior_rows.shape
    ordered = (groups, traces // groups * rows, size)
    laid = (queries.shape[0] + EXTRA, size)
    return pl.pallas_call(
        order_kernel,
        out_shape=[
            jax.ShapeDtypeStruct(ordered, jnp.bfloat16),
            jax.ShapeDtypeStruct(laid, jnp.bfloat16),
        ],
        in_specs=[SMEM, SMEM, HBM, HBM, VMEM],
        out_specs=[HBM, HBM],
        scratch_shapes=[
            pltpu.VMEM((traces, rows, size), jnp.bfloat16),
            pltpu.VMEM((2, rows, size), jnp.float32),
            pltpu.VMEM(ordered, jnp.bfloat16),
            pltpu.VMEM(laid, jnp.bfloat16),
            pltpu.SemaphoreType.DMA((traces,)),
            pltpu.SemaphoreType.DMA((groups,)),
            pltpu.SemaphoreType.DMA((2,)),
        ],
        compiler_params=kernel_params(LARGE),
        cost_estimate=cost(0, 4 * traces * rows * size),
    )(place, slot_trace, prior_rows, queries, reward)


def stage_kernel(place_ref, weight_ref, *refs):
    outs, (staged, kept, in_sems, out_sems) = refs[-8:-4], refs[-4:]
    pools = len(outs)
    size, columns = outs[0].shape
    arriving = []
    for o in range(1, pools):
        to = lax.rem(place_ref[POOL] + pools - o, pools)
        half = weight_ref.at[
            pl.ds(pl.multiple_of(place_ref[CORE] * size, size), size),
            pl.ds(pl.multiple_of(to * columns, columns), columns),
        ]
        arriving.append(pltpu.make_async_copy(half, staged.at[o - 1], in_sems.at[o]))
    own = weight_ref.at[:, pl.ds(pl.multiple_of(place_ref[POOL] * columns, columns), columns)]
    arriving.append(pltpu.make_async_copy(own, kept, in_sems.at[0]))
    for copy in arriving:
        copy.start()
    sources = [staged.at[n] for n in range(pools - 1)] + [kept]
    leaving = [
        pltpu.make_async_copy(source, out, out_sems.at[n])
        for n, (source, out) in enumerate(zip(sources, outs))
    ]
    for n, copy in enumerate(leaving):
        arriving[n].wait()
        copy.start()
    for copy in leaving:
        copy.wait()


def stage(place, weight, pools, behind):
    block = (weight.shape[0] // 2, weight.shape[1] // pools)
    kept = (weight.shape[0], block[1])
    return pl.pallas_call(
        stage_kernel,
        out_shape=[jax.ShapeDtypeStruct(block, jnp.bfloat16)] * (pools - 1)
        + [jax.ShapeDtypeStruct(kept, jnp.bfloat16)],
        in_specs=[SMEM, HBM, HBM],
        out_specs=[HBM] * pools,
        scratch_shapes=[
            pltpu.VMEM((pools - 1, *block), jnp.bfloat16),
            pltpu.VMEM(kept, jnp.bfloat16),
            pltpu.SemaphoreType.DMA((pools,)),
            pltpu.SemaphoreType.DMA((pools,)),
        ],
        compiler_params=kernel_params(LARGE),
        cost_estimate=cost(0, 8 * pools * block[0] * block[1]),
    )(place, weight, behind)


def pack_kernel(
    place_ref, q0, q1, q2, q3, fresh_ref, behind_ref, packed_ref, new_ref, head_ref, wide
):
    slots, rows = packed_ref.shape[1:3]
    head_ref[...] = jnp.zeros_like(head_ref)
    found = []
    for n, ref in enumerate((q0, q1, q2, q3)):
        for slot in range(slots):
            packed_ref[n, slot] = ref[pl.ds(slot * rows, rows), :]
        pieces = ref[pl.ds(slots * rows, EXTRA), :].astype(jnp.float32)
        found += [three_rows(pieces, half) for half in range(2)]
    count = len(found)
    at = pl.ds(pl.multiple_of(place_ref[TP] * count, count), count)
    head_ref[at, :] = rows_of((count, wide.shape[1]), found)
    for slot in range(slots):
        wide[...] = fresh_ref[slot].astype(jnp.float32)
        for kind in range(2):
            part = wide[pl.ds(kind, wide.shape[0] // 2, stride=2), :]
            new_ref[slot, kind] = part.astype(jnp.bfloat16)


def pack(place, queried, fresh, behind, tps):
    pools = len(queried)
    slots, rows, size = fresh.shape
    per_slot = (queried[0].shape[0] - EXTRA) // slots
    return pl.pallas_call(
        pack_kernel,
        out_shape=[
            jax.ShapeDtypeStruct((pools, slots, per_slot, size), jnp.bfloat16),
            jax.ShapeDtypeStruct((slots, 2, rows // 2, size), jnp.bfloat16),
            jax.ShapeDtypeStruct((tps * pools * 2, size), jnp.float32),
        ],
        in_specs=[SMEM] + [VMEM] * (pools + 1) + [HBM],
        out_specs=[VMEM] * 3,
        scratch_shapes=[pltpu.VMEM((rows, size), jnp.float32)],
        compiler_params=kernel_params(8),
        cost_estimate=cost(0, 4 * pools * slots * per_slot * size),
    )(place, *queried, fresh, behind)


def attend_kernel(
    place_ref, trace_ref, length_ref, query_ref, new_ref, prior_ref, weight_ref, head_ref,
    pay_ref, seen_ref, held, sems,
):
    span = held.shape[2]
    copies = []
    for n in range(held.shape[0]):
        start = pl.multiple_of(lax.rem(place_ref[POOL] + n, held.shape[0]) * span, span)
        copies.append(
            pltpu.make_async_copy(weight_ref.at[:, pl.ds(start, span)], held.at[n], sems.at[n])
        )
        copies[-1].start()
    pools, slots, rows, size = query_ref.shape
    sources, block = prior_ref.shape[0], prior_ref.shape[1] // (2 * slots)
    width = sources * block
    factor = size**-0.5 * log2_e
    contract = (((1,), (1,)), ((), ()))
    position = lax.broadcasted_iota(jnp.int32, (1, width), 1)

    def keys_of(slot):
        return prior_ref[:, pl.ds(2 * slot * block, block), :].reshape(width, size)

    def scores_of(slot, tile):
        return lax.dot_general(
            query_ref[tile, slot], keys_of(slot), contract, preferred_element_type=jnp.float32
        )

    ahead = scores_of(0, 0)
    for slot in range(slots):
        valid = length_ref[trace_ref[place_ref[SLOT] + slot]] - place_ref[POOL] * width
        usable = position < valid
        values = prior_ref[:, pl.ds((2 * slot + 1) * block, block), :].reshape(width, size)
        for tile in range(pools):
            pay = pay_ref.at[lax.rem(place_ref[POOL] + tile, pools)]
            query = query_ref[tile, slot]
            scores = ahead
            if tile < pools - 1:
                ahead = scores_of(slot, tile + 1)
            elif slot < slots - 1:
                ahead = scores_of(slot + 1, 0)
            scores = jnp.where(usable, scores, negative_fill)
            peak = jnp.max(scores, -1, keepdims=True)
            if tile == 0:
                fresh_scores = lax.dot_general(
                    query, new_ref[slot, 0], contract, preferred_element_type=jnp.float32
                )
                heads = rows // fresh_scores.shape[1]
                token = lax.broadcasted_iota(jnp.int32, fresh_scores.shape, 0) // heads
                causal = lax.broadcasted_iota(jnp.int32, fresh_scores.shape, 1) <= token
                fresh_scores = jnp.where(causal, fresh_scores, negative_fill)
                peak = jnp.maximum(peak, jnp.max(fresh_scores, -1, keepdims=True))
            peak = jnp.maximum(peak * factor, peak_floor).astype(jnp.bfloat16).astype(jnp.float32)
            weights = jnp.exp2(scores * factor - peak)
            total = jnp.sum(weights, -1, keepdims=True)
            blended = jnp.dot(
                weights.astype(jnp.bfloat16), values, preferred_element_type=jnp.float32
            )
            if tile == 0:
                fresh_weights = jnp.exp2(fresh_scores * factor - peak)
                total = total + jnp.sum(fresh_weights, -1, keepdims=True)
                blended = blended + jnp.dot(
                    fresh_weights.astype(jnp.bfloat16),
                    new_ref[slot, 1],
                    preferred_element_type=jnp.float32,
                )
            pay[pl.ds(slot * rows, rows), :] = blended.astype(jnp.bfloat16)
            high = total.astype(jnp.bfloat16).astype(jnp.float32)
            columns = columns_of((rows, size), (peak, high, total - high))
            halves = [columns[n : n + size].T[:8] for n in range(0, rows, size)]
            pay[pl.ds(slots * rows + slot * EXTRA, EXTRA), :] = jnp.concatenate(halves, 0).astype(
                jnp.bfloat16
            )


    seen = jnp.zeros((held.shape[1], size), jnp.float32)
    for n, copy in enumerate(copies):
        copy.wait()
        for m in range(span // size):
            at = 2 * (m // 2 * pools + n) + m % 2
            part = held[n, :, pl.ds(m * size, size)].astype(jnp.float32)
            seen += part * head_ref[at : at + 1, :]
    column = jnp.sum(seen, -1, keepdims=True)
    for n in range(held.shape[1] // size):
        row = jnp.broadcast_to(column[n * size : (n + 1) * size], (size, size)).T
        seen_ref[pl.ds(4 * n, 4), :] = row[:4]


def attend(place, slot_trace, prefix_length, queries, new, prior, weight, head):
    pools, slots, rows, size = queries.shape
    width = prior.shape[0] * prior.shape[1] // (2 * slots)
    return pl.pallas_call(
        attend_kernel,
        out_shape=[
            jax.ShapeDtypeStruct((pools, slots * (rows + EXTRA), size), jnp.bfloat16),
            jax.ShapeDtypeStruct((4 * weight.shape[0] // size, size), jnp.float32),
        ],
        in_specs=[SMEM] * 3 + [VMEM] * 3 + [HBM, VMEM],
        out_specs=[VMEM] * 2,
        scratch_shapes=[
            pltpu.VMEM((pools, weight.shape[0], weight.shape[1] // pools), jnp.bfloat16),
            pltpu.SemaphoreType.DMA((pools,)),
        ],
        compiler_params=kernel_params(28),
        cost_estimate=cost(32 * rows * width * size, 8 * width * size, 8 * rows * width),
    )(place, slot_trace, prefix_length, queries, new, prior, weight, head)


def columns_of(shape, columns):
    lane = lax.broadcasted_iota(jnp.int32, shape, 1)
    laid = jnp.zeros(shape, jnp.float32)
    for n, column in enumerate(columns):
        laid = jnp.where(lane == n, column, laid)
    return laid


def rows_of(shape, rows):
    at = lax.broadcasted_iota(jnp.int32, shape, 0)
    laid = jnp.zeros(shape, jnp.float32)
    for n, row in enumerate(rows):
        laid = jnp.where(at == n, row, laid)
    return laid


def split_three(value):
    high = value.astype(jnp.bfloat16).astype(jnp.float32)
    middle = (value - high).astype(jnp.bfloat16).astype(jnp.float32)
    return high, middle, value - high - middle


def merge_kernel(pay_ref, seen_ref, out_ref, wide):
    rows, size = wide.shape
    heads = rows // size
    pools = out_ref.shape[0]
    slots = out_ref.shape[1] // rows
    for slot in range(slots):
        peaks, totals = [], []
        for n in range(pools):
            stats = pay_ref[n, pl.ds(slots * rows + slot * EXTRA, EXTRA), :].astype(jnp.float32)
            laid = jnp.concatenate(
                [
                    jnp.concatenate([stats[8 * half : 8 * half + 8]] * (size // 8), 0).T
                    for half in range(heads)
                ],
                0,
            )
            peaks.append(laid[:, 0:1])
            totals.append(laid[:, 1:2] + laid[:, 2:3])
        top = functools.reduce(jnp.maximum, peaks)
        shares = [jnp.exp2(peak - top) for peak in peaks]
        total = sum(share * part for share, part in zip(shares, totals))
        blended = sum(
            share * pay_ref[n, pl.ds(slot * rows, rows), :].astype(jnp.float32)
            for n, share in enumerate(shares)
        )
        wide[...] = blended / total
        for head in range(heads):
            part = wide[pl.ds(head, size, stride=heads), :].astype(jnp.bfloat16)
            for n in range(pools):
                out_ref[n, pl.ds(slot * rows + head * size, size), :] = part
    rewards = []
    for slot in range(slots):
        reward = jnp.zeros((size, 1), jnp.float32)
        for head in range(heads):
            part = out_ref[0, pl.ds(slot * rows + head * size, size), :].astype(jnp.float32)
            reward += jnp.sum(part * seen_ref[4 * head : 4 * head + 1, :], -1, keepdims=True)
        rewards += split_three(reward)
    laid = columns_of((size, size), rewards).T[:EXTRA].astype(jnp.bfloat16)
    for n in range(pools):
        out_ref[n, pl.ds(slots * rows, EXTRA), :] = laid


def merge(pays, seen, slots):
    pools, rows, size = pays.shape
    rows = rows // slots - EXTRA
    return pl.pallas_call(
        merge_kernel,
        out_shape=jax.ShapeDtypeStruct((pools, slots * rows + EXTRA, size), jnp.bfloat16),
        in_specs=[VMEM] * 2,
        out_specs=VMEM,
        scratch_shapes=[pltpu.VMEM((rows, size), jnp.float32)],
        compiler_params=kernel_params(8),
        cost_estimate=cost(0, 20 * rows * size),
    )(pays, seen)


def project_kernel(offsets, place_ref, attended_ref, weight_ref, *refs):
    outs, (weights, sems) = refs[-2 - len(offsets) : -2], refs[-2:]
    moved, wide = refs[: -2 - len(offsets)], outs[0].shape[1]
    dests = weight_ref.shape[1] // wide
    pools, tokens, size = attended_ref.shape[0], outs[0].shape[0] - EXTRA, attended_ref.shape[2]
    slots = tokens // size
    core = place_ref[CORE]
    copies = []
    for i, o in enumerate(offsets):
        dest = lax.rem(place_ref[TP] + o, dests)
        start = pl.ds(pl.multiple_of(dest * wide, wide), wide)
        at = pl.ds(i * wide, wide)
        batch = [(weight_ref.at[:, start], weights.at[0, :, at])]
        for n, ref in enumerate(moved):
            half = core if n % 2 == 0 else 1 - core
            rows = pl.ds(pl.multiple_of(half * size, size), size)
            batch.append((ref.at[pl.ds(0, size), start], weights.at[1 + n // 2, rows, at]))
        copies.append([
            pltpu.make_async_copy(source, target, sems.at[i, n])
            for n, (source, target) in enumerate(batch)
        ])
        for copy in copies[-1]:
            copy.start()
    inputs = []
    for n in range(pools):
        ref = attended_ref.at[lax.rem(place_ref[POOL] + n, pools)]
        rows = [
            jnp.concatenate([ref[pl.ds(at, size), :], ref[pl.ds(at + size, size), :]], 1)
            for at in range(0, 2 * slots * size, 2 * size)
        ]
        inputs.append(jnp.concatenate(rows, 0))
    rewards = jnp.zeros((EXTRA, size), jnp.float32)
    for n in range(pools):
        rewards += attended_ref[n, pl.ds(2 * tokens, EXTRA), :].astype(jnp.float32)
    pieces = []
    for slot in range(slots):
        pieces += split_three(three_rows(rewards, slot))
    laid = rows_of((EXTRA, size), pieces)
    laid = jnp.concatenate([laid, jnp.zeros_like(laid)], 1).astype(jnp.bfloat16)
    for i, out in enumerate(outs):
        out[pl.ds(tokens, EXTRA), :] = laid
        for copy in copies[i]:
            copy.wait()
        at = pl.ds(i * wide, wide)
        total = jnp.dot(inputs[0], weights[0, :, at], preferred_element_type=jnp.float32)
        for n in range(1, pools):
            total += jnp.dot(inputs[n], weights[n, :, at], preferred_element_type=jnp.float32)
        out[pl.ds(0, tokens), :] = total.astype(jnp.bfloat16)


def project(place, attended, weight, moved, dests, offsets):
    pools, rows, size = attended.shape
    tokens = (rows - EXTRA) // 2
    wide = weight.shape[1] // dests
    count = len(offsets)
    return pl.pallas_call(
        functools.partial(project_kernel, offsets),
        out_shape=[jax.ShapeDtypeStruct((tokens + EXTRA, wide), jnp.bfloat16)] * count,
        in_specs=[SMEM, VMEM] + [HBM] * (1 + len(moved)),
        out_specs=[VMEM] * count,
        scratch_shapes=[
            pltpu.VMEM((pools, weight.shape[0], count * wide), jnp.bfloat16),
            pltpu.SemaphoreType.DMA((count, 1 + len(moved))),
        ],
        compiler_params=kernel_params(16),
        cost_estimate=cost(16 * tokens * size * count * wide, 16 * size * count * wide),
    )(place, attended, weight, *moved)


def three_rows(array, slot):
    return sum(array[3 * slot + n : 3 * slot + n + 1] for n in range(3))


def finish_kernel(*refs):
    arrived, (bound_ref, out_ref, reward_ref) = refs[:-3], refs[-3:]
    slots, tokens, wide = out_ref.shape
    steps = bound_ref.shape[1]
    rewards = jnp.zeros((EXTRA, wide), jnp.float32)
    for ref in arrived:
        rewards += ref[pl.ds(slots * tokens, EXTRA), :].astype(jnp.float32)
    for slot in range(slots):
        total = jnp.zeros((tokens, wide), jnp.float32)
        for ref in arrived:
            total += ref[pl.ds(slot * tokens, tokens), :].astype(jnp.float32)
        out_ref[slot] = total.astype(jnp.bfloat16)
        row = jnp.broadcast_to(three_rows(rewards, slot)[:, :tokens], (tokens, tokens)).T[:, :steps]
        lane = lax.broadcasted_iota(jnp.int32, (tokens, steps), 0)
        chosen = jnp.where(lane == bound_ref[slot : slot + 1, :], row, 0.0)
        reward_ref[slot : slot + 1, :] = jnp.sum(chosen, 0, keepdims=True)


def finish(arrived, boundaries):
    slots, steps = boundaries.shape
    rows, wide = arrived[0].shape
    return pl.pallas_call(
        finish_kernel,
        out_shape=[
            jax.ShapeDtypeStruct((slots, (rows - EXTRA) // slots, wide), jnp.bfloat16),
            jax.ShapeDtypeStruct((slots, steps), jnp.float32),
        ],
        in_specs=[VMEM] * (1 + len(arrived)),
        out_specs=[VMEM] * 2,
        compiler_params=kernel_params(8),
    )(*arrived, boundaries)


def shards(
    prior_cache,
    prefix_length,
    slot_trace,
    queries,
    new_token_cache,
    boundaries,
    output_weight,
    reward_weight,
):
    pool, seq, tp = lax.axis_index("pool"), lax.axis_index("seq"), lax.axis_index("tp")
    pools, seqs, tps = lax.axis_size("pool"), lax.axis_size("seq"), lax.axis_size("tp")
    slots, new_len, _, pair, size = queries.shape
    traces, block = prior_cache.shape[:2]
    place = jnp.stack([seq * slots, pool, lax.rem(seq, 2), tp]).astype(jnp.int32)
    rows_all = output_weight.reshape(pair * size, -1)
    prior_rows = prior_cache.reshape(traces, 2 * block, size)
    own_queries = queries.reshape(slots * new_len * pair, size)

    def from_pool(array, offset):
        return lax.ppermute(array, "pool", [((n + offset) % pools, n) for n in range(pools)])

    def turn(array, axes):
        return lax.all_to_all(array, axes, split_axis=0, concat_axis=0, tiled=True)

    def swap_core(array):
        return lax.ppermute(array, "seq", [(n, n ^ 1) for n in range(seqs)])

    sent, own = order_blocks(
        place, slot_trace, prior_rows, own_queries, reward_weight.reshape(-1, size), seqs
    )
    prior = turn(sent, "seq")

    queried = [own] + [from_pool(own, o) for o in range(1, pools)]
    *leaving, kept = stage(place, rows_all, pools, own)
    came = [from_pool(part, o) for o, part in enumerate(leaving, 1)]
    fresh = new_token_cache.reshape(slots, 2 * new_len, size)
    packed, new, head = pack(place, queried, fresh, kept, tps)

    near = [lax.ppermute(head, "tp", [(n, n ^ o) for n in range(tps)]) for o in (1, 2, 3)]
    head = head + near[0] + near[1] + near[2]
    head = head + lax.ppermute(head, "tp", [(n, n ^ 4) for n in range(tps)])

    pays, seen = attend(
        place, slot_trace, prefix_length, packed, new, prior, rows_all, head
    )
    pays, came = lax.optimization_barrier((pays, came))
    moved = [part for got in came for part in (got, swap_core(got))]
    gathered = turn(merge(turn(pays, "pool"), seen, slots), "pool")
    arrived = []
    for offsets in ((4, 3, 5), (2, 6, 1, 7, 0)):
        for o, part in zip(offsets, project(place, gathered, kept, moved, tps, offsets)):
            arrived.append(
                lax.ppermute(part, "tp", [(n, (n + o) % tps) for n in range(tps)]) if o else part
            )
    return tuple(finish(arrived, boundaries))


def solution(mesh):
    placed = (
        P(None, ("pool", "seq"), "tp", None, None),
        P(),
        P(),
        P("seq", None, "tp", "pool", None),
        P("seq", None, "tp", None, None),
        P("seq", None),
        P("tp", "pool", None, None),
        P(("pool", "tp")),
    )
    return jax.shard_map(
        shards,
        mesh=mesh,
        in_specs=placed,
        out_specs=(P("seq", None, ("pool", "tp")), P("seq", None)),
        check_vma=False,
    )
```

```python
import functools

import jax
import jax.numpy as jnp
from jax import lax
from jax.experimental import pallas as pl
from jax.experimental.pallas import tpu as pltpu
from jax.sharding import PartitionSpec as P

negative_fill = -1e30
peak_floor = -1e25
log2_e = 1.4426950408889634
VMEM = pl.BlockSpec(memory_space=pltpu.VMEM)
SMEM = pl.BlockSpec(memory_space=pltpu.SMEM)
HBM = pl.BlockSpec(memory_space=pltpu.HBM)
EXTRA = 16
SLOT, POOL, CORE, TP = range(4)
LARGE = 60


def kernel_params(mib):
    return pltpu.CompilerParams(vmem_limit_bytes=mib * 1024 * 1024)


def cost(flops, moved, exps=0):
    return pl.CostEstimate(flops=flops, bytes_accessed=moved, transcendentals=exps)


def order_kernel(
    place_ref, trace_ref, cache_ref, query_ref, reward_ref, out_ref, leaving_ref,
    held, wide, ordered, laid, sems, out_sems, own_sems,
):
    traces, rows, size = held.shape
    groups = out_ref.shape[0]
    slots = traces // groups
    copies = [
        pltpu.make_async_copy(cache_ref.at[trace_ref[n]], held.at[n], sems.at[n])
        for n in range(traces)
    ]
    for copy in copies:
        copy.start()
    query_rows = query_ref.shape[0]
    query_copy = pltpu.make_async_copy(query_ref, laid.at[pl.ds(0, query_rows), :], own_sems.at[0])
    query_copy.start()
    pieces = split_three(reward_ref[...])
    pieces = [piece[half : half + 1, :] for half in range(2) for piece in pieces]
    laid[pl.ds(query_rows, EXTRA), :] = rows_of((EXTRA, size), pieces).astype(jnp.bfloat16)
    pending = []
    for n, copy in enumerate(copies):
        copy.wait()
        wide[n % 2] = held[n].astype(jnp.float32)
        for kind in range(2):
            part = wide[n % 2, pl.ds(kind, rows // 2, stride=2), :]
            at = n % slots * rows + kind * (rows // 2)
            ordered[n // slots, pl.ds(at, rows // 2), :] = part.astype(jnp.bfloat16)
        if n % slots == slots - 1:
            group = n // slots
            pending.append(
                pltpu.make_async_copy(ordered.at[group], out_ref.at[group], out_sems.at[group])
            )
            pending[-1].start()
        if n == traces // 2:
            query_copy.wait()
            pending.append(pltpu.make_async_copy(laid, leaving_ref, own_sems.at[1]))
            pending[-1].start()
    for copy in pending:
        copy.wait()


def order_blocks(place, slot_trace, prior_rows, queries, reward, groups):
    traces, rows, size = prior_rows.shape
    ordered = (groups, traces // groups * rows, size)
    laid = (queries.shape[0] + EXTRA, size)
    return pl.pallas_call(
        order_kernel,
        out_shape=[
            jax.ShapeDtypeStruct(ordered, jnp.bfloat16),
            jax.ShapeDtypeStruct(laid, jnp.bfloat16),
        ],
        in_specs=[SMEM, SMEM, HBM, HBM, VMEM],
        out_specs=[HBM, HBM],
        scratch_shapes=[
            pltpu.VMEM((traces, rows, size), jnp.bfloat16),
            pltpu.VMEM((2, rows, size), jnp.float32),
            pltpu.VMEM(ordered, jnp.bfloat16),
            pltpu.VMEM(laid, jnp.bfloat16),
            pltpu.SemaphoreType.DMA((traces,)),
            pltpu.SemaphoreType.DMA((groups,)),
            pltpu.SemaphoreType.DMA((2,)),
        ],
        compiler_params=kernel_params(LARGE),
        cost_estimate=cost(0, 4 * traces * rows * size),
    )(place, slot_trace, prior_rows, queries, reward)


def stage_kernel(place_ref, weight_ref, *refs):
    outs, (staged, kept, in_sems, out_sems) = refs[-8:-4], refs[-4:]
    pools = len(outs)
    size, columns = outs[0].shape
    arriving = []
    for o in range(1, pools):
        to = lax.rem(place_ref[POOL] + pools - o, pools)
        half = weight_ref.at[
            pl.ds(pl.multiple_of(place_ref[CORE] * size, size), size),
            pl.ds(pl.multiple_of(to * columns, columns), columns),
        ]
        arriving.append(pltpu.make_async_copy(half, staged.at[o - 1], in_sems.at[o]))
    own = weight_ref.at[:, pl.ds(pl.multiple_of(place_ref[POOL] * columns, columns), columns)]
    arriving.append(pltpu.make_async_copy(own, kept, in_sems.at[0]))
    for copy in arriving:
        copy.start()
    sources = [staged.at[n] for n in range(pools - 1)] + [kept]
    leaving = [
        pltpu.make_async_copy(source, out, out_sems.at[n])
        for n, (source, out) in enumerate(zip(sources, outs))
    ]
    for n, copy in enumerate(leaving):
        arriving[n].wait()
        copy.start()
    for copy in leaving:
        copy.wait()


def stage(place, weight, pools, behind):
    block = (weight.shape[0] // 2, weight.shape[1] // pools)
    kept = (weight.shape[0], block[1])
    return pl.pallas_call(
        stage_kernel,
        out_shape=[jax.ShapeDtypeStruct(block, jnp.bfloat16)] * (pools - 1)
        + [jax.ShapeDtypeStruct(kept, jnp.bfloat16)],
        in_specs=[SMEM, HBM, HBM],
        out_specs=[HBM] * pools,
        scratch_shapes=[
            pltpu.VMEM((pools - 1, *block), jnp.bfloat16),
            pltpu.VMEM(kept, jnp.bfloat16),
            pltpu.SemaphoreType.DMA((pools,)),
            pltpu.SemaphoreType.DMA((pools,)),
        ],
        compiler_params=kernel_params(LARGE),
        cost_estimate=cost(0, 8 * pools * block[0] * block[1]),
    )(place, weight, behind)


def pack_kernel(
    place_ref, q0, q1, q2, q3, fresh_ref, behind_ref, packed_ref, new_ref, head_ref, wide
):
    slots, rows = packed_ref.shape[1:3]
    head_ref[...] = jnp.zeros_like(head_ref)
    found = []
    for n, ref in enumerate((q0, q1, q2, q3)):
        for slot in range(slots):
            packed_ref[n, slot] = ref[pl.ds(slot * rows, rows), :]
        pieces = ref[pl.ds(slots * rows, EXTRA), :].astype(jnp.float32)
        found += [three_rows(pieces, half) for half in range(2)]
    count = len(found)
    at = pl.ds(pl.multiple_of(place_ref[TP] * count, count), count)
    head_ref[at, :] = rows_of((count, wide.shape[1]), found)
    for slot in range(slots):
        wide[...] = fresh_ref[slot].astype(jnp.float32)
        for kind in range(2):
            part = wide[pl.ds(kind, wide.shape[0] // 2, stride=2), :]
            new_ref[slot, kind] = part.astype(jnp.bfloat16)


def pack(place, queried, fresh, behind, tps):
    pools = len(queried)
    slots, rows, size = fresh.shape
    per_slot = (queried[0].shape[0] - EXTRA) // slots
    return pl.pallas_call(
        pack_kernel,
        out_shape=[
            jax.ShapeDtypeStruct((pools, slots, per_slot, size), jnp.bfloat16),
            jax.ShapeDtypeStruct((slots, 2, rows // 2, size), jnp.bfloat16),
            jax.ShapeDtypeStruct((tps * pools * 2, size), jnp.float32),
        ],
        in_specs=[SMEM] + [VMEM] * (pools + 1) + [HBM],
        out_specs=[VMEM] * 3,
        scratch_shapes=[pltpu.VMEM((rows, size), jnp.float32)],
        compiler_params=kernel_params(8),
        cost_estimate=cost(0, 4 * pools * slots * per_slot * size),
    )(place, *queried, fresh, behind)


def attend_kernel(
    place_ref, trace_ref, length_ref, query_ref, new_ref, prior_ref, weight_ref, head_ref,
    pay_ref, seen_ref, held, sems,
):
    span = held.shape[2]
    copies = []
    for n in range(held.shape[0]):
        start = pl.multiple_of(lax.rem(place_ref[POOL] + n, held.shape[0]) * span, span)
        copies.append(
            pltpu.make_async_copy(weight_ref.at[:, pl.ds(start, span)], held.at[n], sems.at[n])
        )
        copies[-1].start()
    pools, slots, rows, size = query_ref.shape
    sources, block = prior_ref.shape[0], prior_ref.shape[1] // (2 * slots)
    width = sources * block
    factor = size**-0.5 * log2_e
    contract = (((1,), (1,)), ((), ()))
    position = lax.broadcasted_iota(jnp.int32, (1, width), 1)

    def keys_of(slot):
        return prior_ref[:, pl.ds(2 * slot * block, block), :].reshape(width, size)

    def scores_of(slot, tile):
        return lax.dot_general(
            query_ref[tile, slot], keys_of(slot), contract, preferred_element_type=jnp.float32
        )

    ahead = scores_of(0, 0)
    for slot in range(slots):
        valid = length_ref[trace_ref[place_ref[SLOT] + slot]] - place_ref[POOL] * width
        usable = position < valid
        values = prior_ref[:, pl.ds((2 * slot + 1) * block, block), :].reshape(width, size)
        values = jnp.concatenate([values, jnp.ones_like(values)], 1)
        for tile in range(pools):
            pay = pay_ref.at[lax.rem(place_ref[POOL] + tile, pools)]
            query = query_ref[tile, slot]
            scores = ahead
            if tile < pools - 1:
                ahead = scores_of(slot, tile + 1)
            elif slot < slots - 1:
                ahead = scores_of(slot + 1, 0)
            scores = jnp.where(usable, scores, negative_fill)
            peak = jnp.max(scores, -1, keepdims=True)
            if tile == 0:
                fresh_scores = lax.dot_general(
                    query, new_ref[slot, 0], contract, preferred_element_type=jnp.float32
                )
                heads = rows // fresh_scores.shape[1]
                token = lax.broadcasted_iota(jnp.int32, fresh_scores.shape, 0) // heads
                causal = lax.broadcasted_iota(jnp.int32, fresh_scores.shape, 1) <= token
                fresh_scores = jnp.where(causal, fresh_scores, negative_fill)
                peak = jnp.maximum(peak, jnp.max(fresh_scores, -1, keepdims=True))
            peak = jnp.maximum(peak * factor, peak_floor).astype(jnp.bfloat16).astype(jnp.float32)
            weights = jnp.exp2(scores * factor - peak)
            blended = jnp.dot(
                weights.astype(jnp.bfloat16), values, preferred_element_type=jnp.float32
            )
            total, blended = blended[:, size : size + 1], blended[:, :size]
            if tile == 0:
                fresh_weights = jnp.exp2(fresh_scores * factor - peak)
                total = total + jnp.sum(fresh_weights, -1, keepdims=True)
                blended = blended + jnp.dot(
                    fresh_weights.astype(jnp.bfloat16),
                    new_ref[slot, 1],
                    preferred_element_type=jnp.float32,
                )
            pay[pl.ds(slot * rows, rows), :] = blended.astype(jnp.bfloat16)
            high = total.astype(jnp.bfloat16).astype(jnp.float32)
            columns = columns_of((rows, size), (peak, high, total - high))
            halves = [columns[n : n + size].T[:8] for n in range(0, rows, size)]
            pay[pl.ds(slots * rows + slot * EXTRA, EXTRA), :] = jnp.concatenate(halves, 0).astype(
                jnp.bfloat16
            )


    seen = jnp.zeros((held.shape[1], size), jnp.float32)
    for n, copy in enumerate(copies):
        copy.wait()
        for m in range(span // size):
            at = 2 * (m // 2 * pools + n) + m % 2
            part = held[n, :, pl.ds(m * size, size)].astype(jnp.float32)
            seen += part * head_ref[at : at + 1, :]
    column = jnp.sum(seen, -1, keepdims=True)
    for n in range(held.shape[1] // size):
        row = jnp.broadcast_to(column[n * size : (n + 1) * size], (size, size)).T
        seen_ref[pl.ds(4 * n, 4), :] = row[:4]


def attend(place, slot_trace, prefix_length, queries, new, prior, weight, head):
    pools, slots, rows, size = queries.shape
    width = prior.shape[0] * prior.shape[1] // (2 * slots)
    return pl.pallas_call(
        attend_kernel,
        out_shape=[
            jax.ShapeDtypeStruct((pools, slots * (rows + EXTRA), size), jnp.bfloat16),
            jax.ShapeDtypeStruct((4 * weight.shape[0] // size, size), jnp.float32),
        ],
        in_specs=[SMEM] * 3 + [VMEM] * 3 + [HBM, VMEM],
        out_specs=[VMEM] * 2,
        scratch_shapes=[
            pltpu.VMEM((pools, weight.shape[0], weight.shape[1] // pools), jnp.bfloat16),
            pltpu.SemaphoreType.DMA((pools,)),
        ],
        compiler_params=kernel_params(28),
        cost_estimate=cost(32 * rows * width * size, 8 * width * size, 8 * rows * width),
    )(place, slot_trace, prefix_length, queries, new, prior, weight, head)


def columns_of(shape, columns):
    lane = lax.broadcasted_iota(jnp.int32, shape, 1)
    laid = jnp.zeros(shape, jnp.float32)
    for n, column in enumerate(columns):
        laid = jnp.where(lane == n, column, laid)
    return laid


def rows_of(shape, rows):
    at = lax.broadcasted_iota(jnp.int32, shape, 0)
    laid = jnp.zeros(shape, jnp.float32)
    for n, row in enumerate(rows):
        laid = jnp.where(at == n, row, laid)
    return laid


def split_three(value):
    high = value.astype(jnp.bfloat16).astype(jnp.float32)
    middle = (value - high).astype(jnp.bfloat16).astype(jnp.float32)
    return high, middle, value - high - middle


def merge_kernel(pay_ref, seen_ref, out_ref, wide):
    rows, size = wide.shape
    heads = rows // size
    pools = out_ref.shape[0]
    slots = out_ref.shape[1] // rows
    for slot in range(slots):
        peaks, totals = [], []
        for n in range(pools):
            stats = pay_ref[n, pl.ds(slots * rows + slot * EXTRA, EXTRA), :].astype(jnp.float32)
            laid = jnp.concatenate(
                [
                    jnp.concatenate([stats[8 * half : 8 * half + 8]] * (size // 8), 0).T
                    for half in range(heads)
                ],
                0,
            )
            peaks.append(laid[:, 0:1])
            totals.append(laid[:, 1:2] + laid[:, 2:3])
        top = functools.reduce(jnp.maximum, peaks)
        shares = [jnp.exp2(peak - top) for peak in peaks]
        total = sum(share * part for share, part in zip(shares, totals))
        blended = sum(
            share * pay_ref[n, pl.ds(slot * rows, rows), :].astype(jnp.float32)
            for n, share in enumerate(shares)
        )
        wide[...] = blended / total
        for head in range(heads):
            part = wide[pl.ds(head, size, stride=heads), :].astype(jnp.bfloat16)
            for n in range(pools):
                out_ref[n, pl.ds(slot * rows + head * size, size), :] = part
    rewards = []
    for slot in range(slots):
        reward = jnp.zeros((size, 1), jnp.float32)
        for head in range(heads):
            part = out_ref[0, pl.ds(slot * rows + head * size, size), :].astype(jnp.float32)
            reward += jnp.sum(part * seen_ref[4 * head : 4 * head + 1, :], -1, keepdims=True)
        rewards += split_three(reward)
    laid = columns_of((size, size), rewards).T[:EXTRA].astype(jnp.bfloat16)
    for n in range(pools):
        out_ref[n, pl.ds(slots * rows, EXTRA), :] = laid


def merge(pays, seen, slots):
    pools, rows, size = pays.shape
    rows = rows // slots - EXTRA
    return pl.pallas_call(
        merge_kernel,
        out_shape=jax.ShapeDtypeStruct((pools, slots * rows + EXTRA, size), jnp.bfloat16),
        in_specs=[VMEM] * 2,
        out_specs=VMEM,
        scratch_shapes=[pltpu.VMEM((rows, size), jnp.float32)],
        compiler_params=kernel_params(8),
        cost_estimate=cost(0, 20 * rows * size),
    )(pays, seen)


def project_kernel(offsets, place_ref, attended_ref, weight_ref, *refs):
    outs, (weights, sems) = refs[-2 - len(offsets) : -2], refs[-2:]
    moved, wide = refs[: -2 - len(offsets)], outs[0].shape[1]
    dests = weight_ref.shape[1] // wide
    pools, tokens, size = attended_ref.shape[0], outs[0].shape[0] - EXTRA, attended_ref.shape[2]
    slots = tokens // size
    core = place_ref[CORE]
    copies = []
    for i, o in enumerate(offsets):
        dest = lax.rem(place_ref[TP] + o, dests)
        start = pl.ds(pl.multiple_of(dest * wide, wide), wide)
        at = pl.ds(i * wide, wide)
        batch = [(weight_ref.at[:, start], weights.at[0, :, at])]
        for n, ref in enumerate(moved):
            half = core if n % 2 == 0 else 1 - core
            rows = pl.ds(pl.multiple_of(half * size, size), size)
            batch.append((ref.at[pl.ds(0, size), start], weights.at[1 + n // 2, rows, at]))
        copies.append([
            pltpu.make_async_copy(source, target, sems.at[i, n])
            for n, (source, target) in enumerate(batch)
        ])
        for copy in copies[-1]:
            copy.start()
    inputs = []
    for n in range(pools):
        ref = attended_ref.at[lax.rem(place_ref[POOL] + n, pools)]
        rows = [
            jnp.concatenate([ref[pl.ds(at, size), :], ref[pl.ds(at + size, size), :]], 1)
            for at in range(0, 2 * slots * size, 2 * size)
        ]
        inputs.append(jnp.concatenate(rows, 0))
    rewards = jnp.zeros((EXTRA, size), jnp.float32)
    for n in range(pools):
        rewards += attended_ref[n, pl.ds(2 * tokens, EXTRA), :].astype(jnp.float32)
    pieces = []
    for slot in range(slots):
        pieces += split_three(three_rows(rewards, slot))
    laid = rows_of((EXTRA, size), pieces)
    laid = jnp.concatenate([laid, jnp.zeros_like(laid)], 1).astype(jnp.bfloat16)
    for i, out in enumerate(outs):
        out[pl.ds(tokens, EXTRA), :] = laid
        for copy in copies[i]:
            copy.wait()
        at = pl.ds(i * wide, wide)
        total = jnp.dot(inputs[0], weights[0, :, at], preferred_element_type=jnp.float32)
        for n in range(1, pools):
            total += jnp.dot(inputs[n], weights[n, :, at], preferred_element_type=jnp.float32)
        out[pl.ds(0, tokens), :] = total.astype(jnp.bfloat16)


def project(place, attended, weight, moved, dests, offsets):
    pools, rows, size = attended.shape
    tokens = (rows - EXTRA) // 2
    wide = weight.shape[1] // dests
    count = len(offsets)
    return pl.pallas_call(
        functools.partial(project_kernel, offsets),
        out_shape=[jax.ShapeDtypeStruct((tokens + EXTRA, wide), jnp.bfloat16)] * count,
        in_specs=[SMEM, VMEM] + [HBM] * (1 + len(moved)),
        out_specs=[VMEM] * count,
        scratch_shapes=[
            pltpu.VMEM((pools, weight.shape[0], count * wide), jnp.bfloat16),
            pltpu.SemaphoreType.DMA((count, 1 + len(moved))),
        ],
        compiler_params=kernel_params(16),
        cost_estimate=cost(16 * tokens * size * count * wide, 16 * size * count * wide),
    )(place, attended, weight, *moved)


def three_rows(array, slot):
    return sum(array[3 * slot + n : 3 * slot + n + 1] for n in range(3))


def finish_kernel(*refs):
    arrived, (bound_ref, out_ref, reward_ref) = refs[:-3], refs[-3:]
    slots, tokens, wide = out_ref.shape
    steps = bound_ref.shape[1]
    rewards = jnp.zeros((EXTRA, wide), jnp.float32)
    for ref in arrived:
        rewards += ref[pl.ds(slots * tokens, EXTRA), :].astype(jnp.float32)
    for slot in range(slots):
        total = jnp.zeros((tokens, wide), jnp.float32)
        for ref in arrived:
            total += ref[pl.ds(slot * tokens, tokens), :].astype(jnp.float32)
        out_ref[slot] = total.astype(jnp.bfloat16)
        row = jnp.broadcast_to(three_rows(rewards, slot)[:, :tokens], (tokens, tokens)).T[:, :steps]
        lane = lax.broadcasted_iota(jnp.int32, (tokens, steps), 0)
        chosen = jnp.where(lane == bound_ref[slot : slot + 1, :], row, 0.0)
        reward_ref[slot : slot + 1, :] = jnp.sum(chosen, 0, keepdims=True)


def finish(arrived, boundaries):
    slots, steps = boundaries.shape
    rows, wide = arrived[0].shape
    return pl.pallas_call(
        finish_kernel,
        out_shape=[
            jax.ShapeDtypeStruct((slots, (rows - EXTRA) // slots, wide), jnp.bfloat16),
            jax.ShapeDtypeStruct((slots, steps), jnp.float32),
        ],
        in_specs=[VMEM] * (1 + len(arrived)),
        out_specs=[VMEM] * 2,
        compiler_params=kernel_params(8),
    )(*arrived, boundaries)


def shards(
    prior_cache,
    prefix_length,
    slot_trace,
    queries,
    new_token_cache,
    boundaries,
    output_weight,
    reward_weight,
):
    pool, seq, tp = lax.axis_index("pool"), lax.axis_index("seq"), lax.axis_index("tp")
    pools, seqs, tps = lax.axis_size("pool"), lax.axis_size("seq"), lax.axis_size("tp")
    slots, new_len, _, pair, size = queries.shape
    traces, block = prior_cache.shape[:2]
    place = jnp.stack([seq * slots, pool, lax.rem(seq, 2), tp]).astype(jnp.int32)
    rows_all = output_weight.reshape(pair * size, -1)
    prior_rows = prior_cache.reshape(traces, 2 * block, size)
    own_queries = queries.reshape(slots * new_len * pair, size)

    def from_pool(array, offset):
        return lax.ppermute(array, "pool", [((n + offset) % pools, n) for n in range(pools)])

    def turn(array, axes):
        return lax.all_to_all(array, axes, split_axis=0, concat_axis=0, tiled=True)

    def swap_core(array):
        return lax.ppermute(array, "seq", [(n, n ^ 1) for n in range(seqs)])

    sent, own = order_blocks(
        place, slot_trace, prior_rows, own_queries, reward_weight.reshape(-1, size), seqs
    )
    prior = turn(sent, "seq")

    queried = [own] + [from_pool(own, o) for o in range(1, pools)]
    *leaving, kept = stage(place, rows_all, pools, own)
    came = [from_pool(part, o) for o, part in enumerate(leaving, 1)]
    fresh = new_token_cache.reshape(slots, 2 * new_len, size)
    packed, new, head = pack(place, queried, fresh, kept, tps)

    near = [lax.ppermute(head, "tp", [(n, n ^ o) for n in range(tps)]) for o in (1, 2, 3)]
    head = head + near[0] + near[1] + near[2]
    head = head + lax.ppermute(head, "tp", [(n, n ^ 4) for n in range(tps)])

    pays, seen = attend(
        place, slot_trace, prefix_length, packed, new, prior, rows_all, head
    )
    pays, came = lax.optimization_barrier((pays, came))
    moved = [part for got in came for part in (got, swap_core(got))]
    gathered = turn(merge(turn(pays, "pool"), seen, slots), "pool")
    arrived = []
    for offsets in ((4, 3, 5), (2, 6, 1, 7, 0)):
        for o, part in zip(offsets, project(place, gathered, kept, moved, tps, offsets)):
            arrived.append(
                lax.ppermute(part, "tp", [(n, (n + o) % tps) for n in range(tps)]) if o else part
            )
    return tuple(finish(arrived, boundaries))


def solution(mesh):
    placed = (
        P(None, ("pool", "seq"), "tp", None, None),
        P(),
        P(),
        P("seq", None, "tp", "pool", None),
        P("seq", None, "tp", None, None),
        P("seq", None),
        P("tp", "pool", None, None),
        P(("pool", "tp")),
    )
    return jax.shard_map(
        shards,
        mesh=mesh,
        in_specs=placed,
        out_specs=(P("seq", None, ("pool", "tp")), P("seq", None)),
        check_vma=False,
    )
```
